512 devices in a mesh: tm: 32 (over y, x, core), space: 16 (over z).
Axes of the slice: x: 4, y: 4, z: 16, core: 2. Of those that a mesh axis runs over, the one named last changes fastest.
Arguments:
- initial: float32 [256, 8, 512], P('space'), may hold values from -6 to 6
- stale_start: float32 [256, 8, 512], P('space'), may hold values from -6 to 6
- guess: float32 [32, 256, 8, 512], P('tm', 'space'), may hold values from -6 to 6
- forcing: float32 [256, 8, 512], P('space'), may hold values from -8 to 8
- wall_class: int32 [256, 8, 512], P('space'), may hold values from 0 to 3
- damping_table: float32 [4], replicated, may hold values from 0.01 to 0.25
- coarse_prop: float32 [512, 512], replicated, may hold values from -1 to 1
Outputs:
- corrected: float32 [32, 256, 8, 512], P('tm', 'space')
- residual_norm: float32 [32], P('tm')
The draws below stay inside these ranges and needn't reach their ends.
All inputs are finite; a program needn't handle non-finite values.
Results may differ from the reference program's by a relative error of at most 0.00015.
Values sent between devices are 32-bit elements; how exact they have to be, the bound alone decides.
A program may use at most 128 MiB of HBM per device.

```python
import math
import jax
import jax.numpy as jnp
from jax import lax

NY = 8
NZ = 512
STEPS = 4
CLASSES = 4
NX = 256
SLICES = 32


def draw_coarse_prop(key, part):
    key = jax.random.fold_in(key, 5)
    first, second = jax.random.split(key)
    diagonal = jax.random.uniform(first, (NZ,), jnp.float32, 0.5, 0.94)
    spread = jnp.clip(jax.random.normal(second, (NZ, NZ), jnp.float32), -4.0, 4.0) * (0.05 / math.sqrt(NZ))
    rows = jnp.arange(NZ)[:, None]
    cols = jnp.arange(NZ)[None, :]
    return jnp.where(rows == cols, diagonal[None, :], spread).astype(jnp.float32)


def draw_forcing(key, part):
    key = jax.random.fold_in(key, 9)
    first, second = jax.random.split(key)
    position = jnp.arange(NX).astype(jnp.float32) / max(NX - 1, 1)
    ramp = 1.0 + 2.0 * position[:, None, None]
    rough = jax.random.uniform(second, (NX, NY, NZ), jnp.float32, 0.5, 2.0)
    base = jnp.clip(jax.random.normal(first, (NX, NY, NZ), jnp.float32), -4.0, 4.0) * 0.3
    return (base * ramp * rough).astype(jnp.float32)


def touch_ends(drawn, own_key, low, high):
    longest = drawn.shape.index(max(drawn.shape))
    spots = []
    for shift in (0, 1):
        where = [jax.random.randint(jax.random.fold_in(own_key, axis), (), 0, length) for axis, length in enumerate(drawn.shape)]
        where[longest] = (where[longest] + shift) % drawn.shape[longest]
        spots.append(tuple(where))
    return drawn.at[spots[0]].set(low).at[spots[1]].set(high)


def block_levels(own_key, extent, cuts, least, high):
    def one(dim, shards_of):
        heights = jax.random.uniform(jax.random.fold_in(jax.random.fold_in(own_key, 6), dim), (shards_of,), jnp.float32, least / len(cuts), high / len(cuts))
        return jnp.repeat(jnp.exp(heights), extent[dim] // shards_of).reshape((-1,) + (1,) * (len(extent) - dim - 1))

    level = one(*cuts[0])
    for cut in cuts[1:]:
        level = level * one(*cut)
    return level


def gaussian(rng, shape, scale, limit, cuts=(), kind=jnp.bfloat16):
    loudness = block_levels(rng, shape, cuts, -0.22, 0.18) if cuts else 1.0
    drawn = jax.random.normal(rng, shape, jnp.float32) * scale * loudness
    return jnp.minimum(jnp.maximum(drawn, -limit), limit).astype(kind)


def setup_inputs(seed: int = 0) -> dict:
    key_list = jax.random.split(jax.random.key(seed), 8)
    initial = gaussian(key_list[0], (NX, NY, NZ), 1.0, 6.0, ((0, 16),), jnp.float32)
    stale_start = gaussian(key_list[1], (NX, NY, NZ), 1.0, 6.0, ((0, 16),), jnp.float32)
    guess = gaussian(key_list[2], (SLICES, NX, NY, NZ), 1.0, 6.0, ((0, 32), (1, 16)), jnp.float32)
    forcing = draw_forcing(jax.random.fold_in(key_list[7], 71), 0)
    wall_class = touch_ends(jax.random.randint(key_list[4], (NX, NY, NZ), 0, CLASSES), jax.random.fold_in(key_list[4], 1), 0, CLASSES - 1).astype(jnp.int32)
    damping_table = jnp.clip(jnp.exp(jax.random.uniform(key_list[5], (CLASSES,), jnp.float32, math.log(0.01), math.log(0.25))), 0.01, 0.25)
    coarse_prop = draw_coarse_prop(jax.random.fold_in(key_list[7], 71), 0)
    return {"initial": initial, "stale_start": stale_start, "guess": guess, "forcing": forcing, "wall_class": wall_class, "damping_table": damping_table, "coarse_prop": coarse_prop}


coupling = 0.12

def damping_field(wall_class, damping_table):
    damping = jnp.zeros(wall_class.shape, damping_table.dtype)
    for class_no in range(CLASSES):
        damping = damping + jnp.where(wall_class == class_no, damping_table[class_no], jnp.zeros((), damping_table.dtype))
    return damping

def advance(field, damping, forcing):
    stream = jnp.roll(field, 1, 0) + jnp.roll(field, -1, 0) - 2.0 * field
    padded_y = jnp.pad(field, ((0, 0), (1, 1), (0, 0)))
    beside_y = padded_y[:, 2:] + padded_y[:, :-2] - 2.0 * field
    padded_z = jnp.pad(field, ((0, 0), (0, 0), (1, 1)))
    beside_z = padded_z[:, :, 2:] + padded_z[:, :, :-2] - 2.0 * field
    return field + coupling * (stream + beside_y + beside_z) - damping * field + forcing

def reference(initial, stale_start, guess, forcing, wall_class, damping_table, coarse_prop):
    damping = damping_field(wall_class, damping_table)

    def sweep(field):
        for sweep_step in range(STEPS):
            field = advance(field, damping, forcing)
        return field
    starts = jnp.concatenate([stale_start[None], guess[:-1]], 0)
    relaxed = lax.map(sweep, starts)
    again = jnp.concatenate([initial[None], relaxed[:-1]], 0)
    residual = lax.map(sweep, again) - relaxed

    def chain(carry, term):
        after = jnp.dot(carry.reshape(-1, NZ), coarse_prop, precision=lax.Precision.HIGHEST).reshape(term.shape) + term
        return (after, after)
    zero = jnp.zeros(initial.shape, residual.dtype)
    final, errors = lax.scan(chain, zero, residual)
    corrected = relaxed + errors
    norms = jnp.sqrt(lax.optimization_barrier(jnp.mean(residual * residual, axis=(1, 2, 3))))
    return (corrected, norms)
```

```python
import functools

import jax
import jax.numpy as jnp
from jax import lax
from jax.experimental import pallas as pl
from jax.experimental.pallas import tpu as pltpu
from jax.sharding import PartitionSpec as P

MESH = pl.DeviceIdType.MESH
COUPLING = 0.12
F32, BF16 = jnp.float32, jnp.bfloat16
NT, NS = 32, 16
X, Y, Z = 16, 8, 512
H = 8
PAD = 4
LOWER, UPPER = 0, 1


def split(value):
    high = value.astype(BF16)
    return high, (value - high.astype(F32)).astype(BF16)


def product(value, high, low):
    first, second = split(value)
    return (
        jnp.dot(first, high, preferred_element_type=F32)
        + jnp.dot(first, low, preferred_element_type=F32)
        + jnp.dot(second, high, preferred_element_type=F32)
    )


def kernel(
    initial, stale, guess, forcing, classes, table, coarse,
    landed, norm,
    levels, force, walls, keep, prop, high, low, outbox, scan, result, beside, partial, gathered,
    local_sem, halo_send, halo_recv, turn_send, turn_recv, back_send, back_recv, own_sem,
    beside_send, beside_recv, norm_send, norm_recv,
):
    tm, sp = lax.axis_index("tm"), lax.axis_index("space")
    up, down = (sp + 1) & (NS - 1), (sp + NS - 1) & (NS - 1)
    last, head = tm == NT - 1, tm == NT - 2

    barrier = pltpu.get_barrier_semaphore()

    def greet(peer, slab):
        pl.semaphore_signal(barrier, inc=1, device_id=(peer, slab), device_id_type=MESH)

    greet(tm, up)
    greet(tm, down)
    for i in range(1, NT):
        greet((tm + i) & (NT - 1), sp)
    for i in range(1, NS):
        greet((tm + NT - 2) & (NT - 1), (sp + i) & (NS - 1))

    own = pl.ds(H, X)
    loads = [
        pltpu.make_async_copy(forcing, force.at[own], local_sem.at[1]),
        pltpu.make_async_copy(classes, walls.at[own], local_sem.at[2]),
        pltpu.make_async_copy(coarse, prop, local_sem.at[3]),
    ]
    field = pltpu.make_async_copy(guess.at[0], levels.at[0, own], local_sem.at[0])

    @pl.when(last)
    def _():
        pltpu.make_async_copy(stale, levels.at[0, own], local_sem.at[0]).start()

    @pl.when(jnp.logical_not(last))
    def _():
        field.start()

    for copy in loads:
        copy.start()
    pltpu.make_async_copy(initial, levels.at[9, own], local_sem.at[4]).start()

    pl.semaphore_wait(barrier, 2 + NT - 1 + NS - 1)

    def halo(source, target, side, index, rows):
        if side == 0:
            here, there, slab = pl.ds(X - rows, rows), pl.ds(H - rows, rows), up
        else:
            here, there, slab = pl.ds(0, rows), pl.ds(H + X, rows), down
        return pltpu.make_async_remote_copy(
            src_ref=source.at[here], dst_ref=target.at[there],
            send_sem=halo_send.at[side, index], recv_sem=halo_recv.at[side, index],
            device_id=(tm, slab), device_id_type=MESH,
        )

    sides = (1, 0)
    for side in sides:
        @pl.when(last)
        def _():
            halo(stale, levels.at[0], side, 0, 8).start()

        @pl.when(jnp.logical_not(last))
        def _():
            halo(guess.at[0], levels.at[0], side, 0, 8).start()

        halo(forcing, force, side, 1, 7).start()
        halo(classes, walls, side, 2, 7).start()

        @pl.when(head)
        def _():
            halo(initial, levels.at[9], side, 3, 4).start()

    loads[2].wait()

    def keep_split(power, rows, value):
        first, second = split(value)
        high[power, rows, :] = first
        low[power, rows, :] = second

    def start_power(i, carry):
        rows = pl.ds(pl.multiple_of(i * 128, 128), 128)
        keep_split(0, rows, prop[rows, :])
        return carry

    lax.fori_loop(0, Z // 128, start_power, 0)
    for power in range(1, 4):
        def square(i, carry):
            rows = pl.ds(pl.multiple_of(i * 128, 128), 128)
            first, second = high[power - 1, rows, :], low[power - 1, rows, :]
            value = (
                jnp.dot(first, high[power - 1], preferred_element_type=F32)
                + jnp.dot(first, low[power - 1], preferred_element_type=F32)
                + jnp.dot(second, high[power - 1], preferred_element_type=F32)
            )
            keep_split(power, rows, value)
            return carry

        lax.fori_loop(0, Z // 128, square, 0)

    lane = lax.broadcasted_iota(jnp.int32, (1, Y, Z), 2)
    row = lax.broadcasted_iota(jnp.int32, (1, Y, Z), 1)
    not_left, not_right = lane > 0, lane < Z - 1
    not_first, not_final = row > 0, row < Y - 1

    def keep_factor(start, count):
        def one(i, carry):
            wall = walls[start + i]
            damping = jnp.zeros((Y, Z), F32)
            for class_no in range(4):
                damping = jnp.where(wall == class_no, table[class_no], damping)
            keep[start + i] = (1.0 - 6.0 * COUPLING) - damping
            return carry

        lax.fori_loop(0, count, one, 0)

    second_source = jnp.where(head, 9, 4)

    def step(level, start, count):
        source = second_source if level == 5 else level - 1

        def rows(at, size):
            field = levels[source, pl.ds(at, size)]
            around = levels[source, pl.ds(at - 1, size)] + levels[source, pl.ds(at + 1, size)]
            around += jnp.where(not_left, pltpu.roll(field, 1, 2), 0.0)
            around += jnp.where(not_right, pltpu.roll(field, Z - 1, 2), 0.0)
            around += jnp.where(not_first, pltpu.roll(field, 1, 1), 0.0)
            around += jnp.where(not_final, pltpu.roll(field, Y - 1, 1), 0.0)
            levels[level, pl.ds(at, size)] = (
                field * keep[pl.ds(at, size)] + COUPLING * around + force[pl.ds(at, size)]
            )

        pair = 2

        def one(i, carry):
            rows(start + i * pair, pair)
            return carry

        lax.fori_loop(0, count // pair, one, 0)

    def wait_halo(side):
        for index, (buffer, count) in enumerate(((levels.at[0], 8), (force, 7), (walls, 7))):
            there = pl.ds(H - count, count) if side == 0 else pl.ds(H + X, count)
            pltpu.make_async_copy(buffer.at[there], buffer.at[there], halo_recv.at[side, index]).wait()

        @pl.when(head)
        def _():
            there = pl.ds(H - 4, 4) if side == 0 else pl.ds(H + X, 4)
            pltpu.make_async_copy(levels.at[9, there], levels.at[9, there], halo_recv.at[side, 3]).wait()

    def half_rows(half):
        return pl.ds(H + half * 8, 8)

    def send_half(half):
        pltpu.make_async_remote_copy(
            src_ref=levels.at[4, half_rows(half)], dst_ref=beside.at[half],
            send_sem=beside_send.at[half], recv_sem=beside_recv.at[half],
            device_id=((tm + NT - 1) & (NT - 1), sp), device_id_type=MESH,
        ).start()
        relaxed = levels[4, half_rows(half)].reshape(64, Z)
        carried = product(relaxed, high[0], low[0]).reshape(8, Y, Z)
        term = levels[8, half_rows(half)] - jnp.where(head, 0.0, carried)
        for x in range(8):
            for k in range(4):
                outbox[half, pl.ds(x * 32 + k, 8, stride=4), :] = term[x, :, k * 128 : (k + 1) * 128]
        place = (tm + 2) & (NT - 1)
        pltpu.make_async_copy(
            outbox.at[half, pl.ds(pl.multiple_of(tm * 8, 8), 8)],
            scan.at[half, 0, pl.ds(pl.multiple_of((place + PAD) * 8, 8), 8)],
            own_sem.at[half, 0],
        ).start()
        for i in range(1, NT):
            peer = (tm + i) & (NT - 1)
            pltpu.make_async_remote_copy(
                src_ref=outbox.at[half, pl.ds(pl.multiple_of(peer * 8, 8), 8)],
                dst_ref=scan.at[half, 0, pl.ds(pl.multiple_of((place + PAD) * 8, 8), 8)],
                send_sem=turn_send.at[half], recv_sem=turn_recv.at[half],
                device_id=(peer, sp), device_id_type=MESH,
            ).start()

    for copy in (field, *loads[:2]):
        copy.wait()
    pltpu.make_async_copy(initial, levels.at[9, own], local_sem.at[4]).wait()
    for half in range(2):
        for stage in range(3):
            scan[half, stage, 0 : PAD * 8, :] = jnp.zeros((PAD * 8, 128), F32)
    keep_factor(H, X)
    for level in range(1, 8):
        step(level, H + level, X - 2 * level)
    wait_halo(1)
    keep_factor(H + X, 7)
    for level in range(1, 9):
        step(level, H + X - level, 8)
    send_half(UPPER)
    wait_halo(0)
    keep_factor(1, 7)
    for level in range(1, 9):
        step(level, level, 8)
    send_half(LOWER)

    total = jnp.zeros((Y, Z), F32)
    for half in (UPPER, LOWER):
        pltpu.make_async_copy(beside.at[half], beside.at[half], beside_recv.at[half]).wait()

        def add(i, sums):
            residual = levels[8, H + half * 8 + i] - beside[half, i]
            return sums + residual * residual

        total = lax.fori_loop(0, 8, add, total)
    lanes = total[:, 0:128] + total[:, 128:256] + total[:, 256:384] + total[:, 384:512]
    partial[...] = jnp.sum(lanes, axis=0, keepdims=True)
    for i in range(NS):
        pltpu.make_async_remote_copy(
            src_ref=partial, dst_ref=gathered.at[sp], send_sem=norm_send, recv_sem=norm_recv,
            device_id=((tm + 2) & (NT - 1), (sp + i) & (NS - 1)), device_id_type=MESH,
        ).start()

    def view(half, stage, first, slices):
        pieces = [
            scan[half, stage, pl.ds(first * 8 + k, slices * 2, stride=4), :] for k in range(4)
        ]
        return jnp.concatenate(pieces, axis=1)

    def store(buffer, first, slices, value):
        for k in range(4):
            buffer[pl.ds(first * 8 + k, slices * 2, stride=4), :] = value[:, k * 128 : (k + 1) * 128]

    for half in (UPPER, LOWER):
        mine = outbox.at[half, pl.ds(0, 8)]
        pltpu.make_async_copy(mine, mine, own_sem.at[half, 0]).wait()
        others = outbox.at[half, pl.ds(0, (NT - 1) * 8)]
        pltpu.make_async_copy(others, others, turn_recv.at[half]).wait()
        for stage in range(3):
            after = view(half, stage, PAD, NT) + product(
                view(half, stage, PAD - (1 << stage), NT), high[stage], low[stage]
            )
            if stage < 2:
                store(scan.at[half, stage + 1], PAD, NT, after)
        chunk = after[0:16]
        chunks = [chunk]
        for c in range(1, 4):
            chunk = after[c * 16 : (c + 1) * 16] + product(chunk, high[3], low[3])
            chunks.append(chunk)
        store(result.at[half], 0, NT, jnp.concatenate(chunks, axis=0))
        here = landed.at[pl.ds(pl.multiple_of(half * 256 + tm * 8, 8), 8)]
        pltpu.make_async_copy(
            result.at[half, pl.ds(pl.multiple_of(tm * 8, 8), 8)], here, own_sem.at[half, 1]
        ).start()
        for i in range(1, NT):
            peer = (tm + i) & (NT - 1)
            pltpu.make_async_remote_copy(
                src_ref=result.at[half, pl.ds(pl.multiple_of(peer * 8, 8), 8)], dst_ref=here,
                send_sem=back_send.at[half], recv_sem=back_recv.at[half],
                device_id=(peer, sp), device_id_type=MESH,
            ).start()

    pltpu.make_async_copy(gathered, gathered, norm_recv).wait()
    squares = jnp.sum(gathered[...], axis=0)
    mean = jnp.sum(squares, axis=1, keepdims=True) / (NS * X * Y * Z)
    norm[...] = jnp.broadcast_to(jnp.sqrt(mean), (8, 128))

    for half in range(2):
        mine = outbox.at[half, pl.ds(0, 8)]
        others = outbox.at[half, pl.ds(0, (NT - 1) * 8)]
        pltpu.make_async_copy(mine, mine, own_sem.at[half, 1]).wait()
        pltpu.make_async_copy(others, others, back_recv.at[half]).wait()
        pltpu.make_async_copy(others, others, turn_send.at[half]).wait()
        pltpu.make_async_copy(others, others, back_send.at[half]).wait()
        pltpu.make_async_copy(beside.at[half], beside.at[half], beside_send.at[half]).wait()
    pltpu.make_async_copy(gathered, gathered, norm_send).wait()
    for side in sides:
        for index, (buffer, count) in enumerate(((levels.at[0], 8), (force, 7), (walls, 7))):
            there = pl.ds(0, count)
            pltpu.make_async_copy(buffer.at[there], buffer.at[there], halo_send.at[side, index]).wait()

        @pl.when(head)
        def _():
            there = pl.ds(0, 4)
            pltpu.make_async_copy(levels.at[9, there], levels.at[9, there], halo_send.at[side, 3]).wait()


def shards(initial, stale_start, guess, forcing, wall_class, damping_table, coarse_prop):
    anywhere = pl.BlockSpec(memory_space=pl.ANY)
    dma = pltpu.SemaphoreType.DMA
    landed, norm = pl.pallas_call(
        kernel,
        out_shape=(
            jax.ShapeDtypeStruct((X * Y * Z // 128, 128), F32),
            jax.ShapeDtypeStruct((8, 128), F32),
        ),
        in_specs=[anywhere] * 5 + [pl.BlockSpec(memory_space=pltpu.SMEM), anywhere],
        out_specs=(anywhere, pl.BlockSpec(memory_space=pltpu.VMEM)),
        scratch_shapes=[
            pltpu.VMEM((10, X + 2 * H, Y, Z), F32),
            pltpu.VMEM((X + 2 * H, Y, Z), F32),
            pltpu.VMEM((X + 2 * H, Y, Z), jnp.int32),
            pltpu.VMEM((X + 2 * H, Y, Z), F32),
            pltpu.VMEM((Z, Z), F32),
            pltpu.VMEM((4, Z, Z), BF16),
            pltpu.VMEM((4, Z, Z), BF16),
            pltpu.VMEM((2, NT * 8, 128), F32),
            pltpu.VMEM((2, 3, (PAD + NT) * 8, 128), F32),
            pltpu.VMEM((2, NT * 8, 128), F32),
            pltpu.VMEM((2, 8, Y, Z), F32),
            pltpu.VMEM((1, 128), F32),
            pltpu.VMEM((NS, 1, 128), F32),
            dma((5,)), dma((2, 4)), dma((2, 4)), dma((2,)), dma((2,)), dma((2,)), dma((2,)),
            dma((2, 2)), dma((2,)), dma((2,)), dma, dma,
        ],
        compiler_params=pltpu.CompilerParams(
            collective_id=0, has_side_effects=True, vmem_limit_bytes=48 * 1024 * 1024
        ),
    )(initial, stale_start, guess, forcing, wall_class, damping_table, coarse_prop)
    return landed.reshape(1, X, Y, Z), norm[0, 0:1]


def solution(mesh):
    return jax.shard_map(
        shards,
        mesh=mesh,
        in_specs=(
            P("space", None, None),
            P("space", None, None),
            P("tm", "space", None, None),
            P("space", None, None),
            P("space", None, None),
            P(),
            P(),
        ),
        out_specs=(P("tm", "space", None, None), P("tm")),
        check_vma=False,
    )
```

```python
import functools

import jax
import jax.numpy as jnp
from jax import lax
from jax.experimental import pallas as pl
from jax.experimental.pallas import tpu as pltpu
from jax.sharding import PartitionSpec as P

MESH = pl.DeviceIdType.MESH
COUPLING = 0.12
F32, BF16 = jnp.float32, jnp.bfloat16
NT, NS = 32, 16
X, Y, Z = 16, 8, 512
H = 8
PAD = 4
LOWER, UPPER = 0, 1


def split(value):
    high = value.astype(BF16)
    return high, (value - high.astype(F32)).astype(BF16)


def product(value, high, low):
    first, second = split(value)
    return (
        jnp.dot(first, high, preferred_element_type=F32)
        + jnp.dot(first, low, preferred_element_type=F32)
        + jnp.dot(second, high, preferred_element_type=F32)
    )


def kernel(
    initial, stale, guess, forcing, classes, damping_table, coarse,
    landed, norm,
    table, levels, force, walls, keep, prop, high, low, outbox, scan, result, beside, partial, gathered,
    local_sem, halo_send, halo_recv, turn_send, turn_recv, back_send, back_recv, own_sem,
    beside_send, beside_recv, norm_send, norm_recv, known,
):
    tm, sp = lax.axis_index("tm"), lax.axis_index("space")
    up, down = (sp + 1) & (NS - 1), (sp + NS - 1) & (NS - 1)
    last, head = tm == NT - 1, tm == NT - 2

    barrier = pltpu.get_barrier_semaphore()

    def greet(peer, slab):
        pl.semaphore_signal(barrier, inc=1, device_id=(peer, slab), device_id_type=MESH)

    greet(tm, up)
    greet(tm, down)
    for i in range(1, NT):
        greet((tm + i) & (NT - 1), sp)

    own = pl.ds(H, X)
    loads = [
        pltpu.make_async_copy(forcing, force.at[own], local_sem.at[1]),
        pltpu.make_async_copy(classes, walls.at[own], local_sem.at[2]),
        pltpu.make_async_copy(coarse, prop, local_sem.at[3]),
    ]
    field = pltpu.make_async_copy(guess.at[0], levels.at[0, own], local_sem.at[0])

    @pl.when(last)
    def _():
        pltpu.make_async_copy(stale, levels.at[0, own], local_sem.at[0]).start()

    @pl.when(jnp.logical_not(last))
    def _():
        field.start()

    copy_table = pltpu.make_async_copy(damping_table, table, local_sem.at[5])
    copy_table.start()
    for copy in loads:
        copy.start()
    pltpu.make_async_copy(initial, levels.at[9, own], local_sem.at[4]).start()

    pl.semaphore_wait(barrier, 2 + NT - 1)

    def tell(round_no):
        for way in (1, -1)[: 1 if round_no == 3 else 2]:
            pl.semaphore_signal(
                known.at[round_no], inc=1,
                device_id=(tm, (sp + NS + (way << round_no)) & (NS - 1)), device_id_type=MESH,
            )

    def hear(round_no):
        pl.semaphore_wait(known.at[round_no], 1 if round_no == 3 else 2)

    def halo(source, target, side, index, rows):
        if side == 0:
            here, there, slab = pl.ds(X - rows, rows), pl.ds(H - rows, rows), up
        else:
            here, there, slab = pl.ds(0, rows), pl.ds(H + X, rows), down
        return pltpu.make_async_remote_copy(
            src_ref=source.at[here], dst_ref=target.at[there],
            send_sem=halo_send.at[side, index], recv_sem=halo_recv.at[side, index],
            device_id=(tm, slab), device_id_type=MESH,
        )

    sides = (1, 0)
    for side in sides:
        @pl.when(last)
        def _():
            halo(stale, levels.at[0], side, 0, 8).start()

        @pl.when(jnp.logical_not(last))
        def _():
            halo(guess.at[0], levels.at[0], side, 0, 8).start()

        halo(forcing, force, side, 1, 7).start()
        halo(classes, walls, side, 2, 7).start()

        @pl.when(head)
        def _():
            halo(initial, levels.at[9], side, 3, 4).start()

    tell(0)

    loads[2].wait()

    def keep_split(power, rows, value):
        first, second = split(value)
        high[power, rows, :] = first
        low[power, rows, :] = second

    def start_power(i, carry):
        rows = pl.ds(pl.multiple_of(i * 128, 128), 128)
        keep_split(0, rows, prop[rows, :])
        return carry

    lax.fori_loop(0, Z // 128, start_power, 0)
    for power in range(1, 4):
        def square(i, carry):
            rows = pl.ds(pl.multiple_of(i * 128, 128), 128)
            first, second = high[power - 1, rows, :], low[power - 1, rows, :]
            value = (
                jnp.dot(first, high[power - 1], preferred_element_type=F32)
                + jnp.dot(first, low[power - 1], preferred_element_type=F32)
                + jnp.dot(second, high[power - 1], preferred_element_type=F32)
            )
            keep_split(power, rows, value)
            return carry

        lax.fori_loop(0, Z // 128, square, 0)

    lane = lax.broadcasted_iota(jnp.int32, (1, Y, Z), 2)
    row = lax.broadcasted_iota(jnp.int32, (1, Y, Z), 1)
    not_left, not_right = lane > 0, lane < Z - 1
    not_first, not_final = row > 0, row < Y - 1

    def keep_factor(start, count):
        def one(i, carry):
            wall = walls[start + i]
            damping = jnp.zeros((Y, Z), F32)
            for class_no in range(4):
                damping = jnp.where(wall == class_no, table[class_no], damping)
            keep[start + i] = (1.0 - 6.0 * COUPLING) - damping
            return carry

        lax.fori_loop(0, count, one, 0)

    second_source = jnp.where(head, 9, 4)

    def step(level, start, count):
        source = second_source if level == 5 else level - 1

        def rows(at, size):
            field = levels[source, pl.ds(at, size)]
            around = levels[source, pl.ds(at - 1, size)] + levels[source, pl.ds(at + 1, size)]
            around += jnp.where(not_left, pltpu.roll(field, 1, 2), 0.0)
            around += jnp.where(not_right, pltpu.roll(field, Z - 1, 2), 0.0)
            around += jnp.where(not_first, pltpu.roll(field, 1, 1), 0.0)
            around += jnp.where(not_final, pltpu.roll(field, Y - 1, 1), 0.0)
            levels[level, pl.ds(at, size)] = (
                field * keep[pl.ds(at, size)] + COUPLING * around + force[pl.ds(at, size)]
            )

        for i in range(0, count, 4):
            rows(start + i, min(4, count - i))

    def wait_halo(side):
        for index, (buffer, count) in enumerate(((levels.at[0], 8), (force, 7), (walls, 7))):
            there = pl.ds(H - count, count) if side == 0 else pl.ds(H + X, count)
            pltpu.make_async_copy(buffer.at[there], buffer.at[there], halo_recv.at[side, index]).wait()

        @pl.when(head)
        def _():
            there = pl.ds(H - 4, 4) if side == 0 else pl.ds(H + X, 4)
            pltpu.make_async_copy(levels.at[9, there], levels.at[9, there], halo_recv.at[side, 3]).wait()

    def half_rows(half):
        return pl.ds(H + half * 8, 8)

    def send_half(half):
        pltpu.make_async_remote_copy(
            src_ref=levels.at[4, half_rows(half)], dst_ref=beside.at[half],
            send_sem=beside_send.at[half], recv_sem=beside_recv.at[half],
            device_id=((tm + NT - 1) & (NT - 1), sp), device_id_type=MESH,
        ).start()
        relaxed = levels[4, half_rows(half)].reshape(64, Z)
        carried = product(relaxed, high[0], low[0]).reshape(8, Y, Z)
        term = levels[8, half_rows(half)] - jnp.where(head, 0.0, carried)
        for x in range(8):
            for k in range(4):
                outbox[half, pl.ds(x * 32 + k, 8, stride=4), :] = term[x, :, k * 128 : (k + 1) * 128]
        place = (tm + 2) & (NT - 1)
        pltpu.make_async_copy(
            outbox.at[half, pl.ds(pl.multiple_of(tm * 8, 8), 8)],
            scan.at[half, 0, pl.ds(pl.multiple_of((place + PAD) * 8, 8), 8)],
            own_sem.at[half, 0],
        ).start()
        for i in range(1, NT):
            peer = (tm + i) & (NT - 1)
            pltpu.make_async_remote_copy(
                src_ref=outbox.at[half, pl.ds(pl.multiple_of(peer * 8, 8), 8)],
                dst_ref=scan.at[half, 0, pl.ds(pl.multiple_of((place + PAD) * 8, 8), 8)],
                send_sem=turn_send.at[half], recv_sem=turn_recv.at[half],
                device_id=(peer, sp), device_id_type=MESH,
            ).start()

    for copy in (copy_table, field, *loads[:2]):
        copy.wait()
    pltpu.make_async_copy(initial, levels.at[9, own], local_sem.at[4]).wait()
    for half in range(2):
        for stage in range(3):
            scan[half, stage, 0 : PAD * 8, :] = jnp.zeros((PAD * 8, 128), F32)
    keep_factor(H, X)
    for level in range(1, 8):
        step(level, H + level, X - 2 * level)
    hear(0)
    tell(1)
    wait_halo(1)
    keep_factor(H + X, 7)
    for level in range(1, 9):
        step(level, H + X - level, 8)
    send_half(UPPER)
    hear(1)
    tell(2)
    wait_halo(0)
    keep_factor(1, 7)
    for level in range(1, 9):
        step(level, level, 8)
    send_half(LOWER)
    hear(2)
    tell(3)

    total = jnp.zeros((Y, Z), F32)
    for half in (UPPER, LOWER):
        pltpu.make_async_copy(beside.at[half], beside.at[half], beside_recv.at[half]).wait()

        def add(i, sums):
            residual = levels[8, H + half * 8 + i] - beside[half, i]
            return sums + residual * residual

        total = lax.fori_loop(0, 8, add, total)
    lanes = total[:, 0:128] + total[:, 128:256] + total[:, 256:384] + total[:, 384:512]
    partial[...] = jnp.sum(lanes, axis=0, keepdims=True)
    hear(3)
    for i in range(NS):
        pltpu.make_async_remote_copy(
            src_ref=partial, dst_ref=gathered.at[sp], send_sem=norm_send, recv_sem=norm_recv,
            device_id=((tm + 2) & (NT - 1), (sp + i) & (NS - 1)), device_id_type=MESH,
        ).start()

    def view(half, stage, first, slices):
        pieces = [
            scan[half, stage, pl.ds(first * 8 + k, slices * 2, stride=4), :] for k in range(4)
        ]
        return jnp.concatenate(pieces, axis=1)

    def store(buffer, first, slices, value):
        for k in range(4):
            buffer[pl.ds(first * 8 + k, slices * 2, stride=4), :] = value[:, k * 128 : (k + 1) * 128]

    for half in (UPPER, LOWER):
        mine = outbox.at[half, pl.ds(0, 8)]
        pltpu.make_async_copy(mine, mine, own_sem.at[half, 0]).wait()
        others = outbox.at[half, pl.ds(0, (NT - 1) * 8)]
        pltpu.make_async_copy(others, others, turn_recv.at[half]).wait()
        for stage in range(3):
            after = view(half, stage, PAD, NT) + product(
                view(half, stage, PAD - (1 << stage), NT), high[stage], low[stage]
            )
            if stage < 2:
                store(scan.at[half, stage + 1], PAD, NT, after)
        chunk = after[0:16]
        chunks = [chunk]
        for c in range(1, 4):
            chunk = after[c * 16 : (c + 1) * 16] + product(chunk, high[3], low[3])
            chunks.append(chunk)
        store(result.at[half], 0, NT, jnp.concatenate(chunks, axis=0))
        here = landed.at[pl.ds(pl.multiple_of(half * 256 + tm * 8, 8), 8)]
        pltpu.make_async_copy(
            result.at[half, pl.ds(pl.multiple_of(tm * 8, 8), 8)], here, own_sem.at[half, 1]
        ).start()
        for i in range(1, NT):
            peer = (tm + i) & (NT - 1)
            pltpu.make_async_remote_copy(
                src_ref=result.at[half, pl.ds(pl.multiple_of(peer * 8, 8), 8)], dst_ref=here,
                send_sem=back_send.at[half], recv_sem=back_recv.at[half],
                device_id=(peer, sp), device_id_type=MESH,
            ).start()

    pltpu.make_async_copy(gathered, gathered, norm_recv).wait()
    squares = jnp.sum(gathered[...], axis=0)
    mean = jnp.sum(squares, axis=1, keepdims=True) / (NS * X * Y * Z)
    norm[...] = jnp.broadcast_to(jnp.sqrt(mean), (8, 128))

    for half in range(2):
        mine = outbox.at[half, pl.ds(0, 8)]
        others = outbox.at[half, pl.ds(0, (NT - 1) * 8)]
        pltpu.make_async_copy(mine, mine, own_sem.at[half, 1]).wait()
        pltpu.make_async_copy(others, others, back_recv.at[half]).wait()
        pltpu.make_async_copy(others, others, turn_send.at[half]).wait()
        pltpu.make_async_copy(others, others, back_send.at[half]).wait()
        pltpu.make_async_copy(beside.at[half], beside.at[half], beside_send.at[half]).wait()
    pltpu.make_async_copy(gathered, gathered, norm_send).wait()
    for side in sides:
        for index, (buffer, count) in enumerate(((levels.at[0], 8), (force, 7), (walls, 7))):
            there = pl.ds(0, count)
            pltpu.make_async_copy(buffer.at[there], buffer.at[there], halo_send.at[side, index]).wait()

        @pl.when(head)
        def _():
            there = pl.ds(0, 4)
            pltpu.make_async_copy(levels.at[9, there], levels.at[9, there], halo_send.at[side, 3]).wait()


def shards(initial, stale_start, guess, forcing, wall_class, damping_table, coarse_prop):
    anywhere = pl.BlockSpec(memory_space=pl.ANY)
    hbm = pl.BlockSpec(memory_space=pltpu.HBM)
    dma = pltpu.SemaphoreType.DMA
    landed, norm = pl.pallas_call(
        kernel,
        out_shape=(
            jax.ShapeDtypeStruct((X * Y * Z // 128, 128), F32),
            jax.ShapeDtypeStruct((8, 128), F32),
        ),
        in_specs=[hbm] * 7,
        out_specs=(anywhere, pl.BlockSpec(memory_space=pltpu.VMEM)),
        scratch_shapes=[
            pltpu.SMEM((4,), F32),
            pltpu.VMEM((10, X + 2 * H, Y, Z), F32),
            pltpu.VMEM((X + 2 * H, Y, Z), F32),
            pltpu.VMEM((X + 2 * H, Y, Z), jnp.int32),
            pltpu.VMEM((X + 2 * H, Y, Z), F32),
            pltpu.VMEM((Z, Z), F32),
            pltpu.VMEM((4, Z, Z), BF16),
            pltpu.VMEM((4, Z, Z), BF16),
            pltpu.VMEM((2, NT * 8, 128), F32),
            pltpu.VMEM((2, 3, (PAD + NT) * 8, 128), F32),
            pltpu.VMEM((2, NT * 8, 128), F32),
            pltpu.VMEM((2, 8, Y, Z), F32),
            pltpu.VMEM((1, 128), F32),
            pltpu.VMEM((NS, 1, 128), F32),
            dma((6,)), dma((2, 4)), dma((2, 4)), dma((2,)), dma((2,)), dma((2,)), dma((2,)),
            dma((2, 2)), dma((2,)), dma((2,)), dma, dma, pltpu.SemaphoreType.REGULAR((4,)),
        ],
        compiler_params=pltpu.CompilerParams(
            collective_id=0, has_side_effects=True, vmem_limit_bytes=63 * 1024 * 1024
        ),
    )(initial, stale_start, guess, forcing, wall_class, damping_table, coarse_prop)
    return landed.reshape(1, X, Y, Z), norm[0, 0:1]


def solution(mesh):
    return jax.shard_map(
        shards,
        mesh=mesh,
        in_specs=(
            P("space", None, None),
            P("space", None, None),
            P("tm", "space", None, None),
            P("space", None, None),
            P("space", None, None),
            P(),
            P(),
        ),
        out_specs=(P("tm", "space", None, None), P("tm")),
        check_vma=False,
    )
```

```python
import functools

import jax
import jax.numpy as jnp
from jax import lax
from jax.experimental import pallas as pl
from jax.experimental.pallas import tpu as pltpu
from jax.sharding import PartitionSpec as P

MESH = pl.DeviceIdType.MESH
COUPLING = 0.12
F32, BF16 = jnp.float32, jnp.bfloat16
NT, NS = 32, 16
X, Y, Z = 16, 8, 512
MIDDLE = 4
H = 8
PAD = 4
BLOCK = 256
LOWER, UPPER = 0, 1


def split(value):
    high = value.astype(BF16)
    return high, (value - high.astype(F32)).astype(BF16)


def product(value, high, low):
    first, second = split(value)
    return (
        jnp.dot(first, high, preferred_element_type=F32)
        + jnp.dot(first, low, preferred_element_type=F32)
        + jnp.dot(second, high, preferred_element_type=F32)
    )


def moved(tm, dy, dx, dc):
    return ((tm + 8 * dy) & 24) | ((tm + 2 * dx) & 6) | ((tm ^ dc) & 1)


PEERS = sorted(
    [(dy, dx, dc) for dy in range(4) for dx in range(4) for dc in range(2)][1:],
    key=lambda d: -min(d[0], 4 - d[0]) - min(d[1], 4 - d[1]),
)
LINE = [(0, dx, dc) for dx in range(4) for dc in range(2)][1:]
BESIDE = LINE + [(dy, 0, dc) for dy in range(1, 4) for dc in range(2)]


def kernel(
    initial, stale, guess, forcing, classes, damping_table, coarse,
    landed, norm,
    table, levels, force, walls, keep, prop, high, low, outbox, scan, result, beside, partial, gathered,
    local_sem, halo_send, halo_recv, turn_send, turn_recv, back_send, back_recv, own_sem,
    beside_send, beside_recv, norm_send, norm_recv, known,
):
    tm, sp = lax.axis_index("tm"), lax.axis_index("space")
    up, down = (sp + 1) & (NS - 1), (sp + NS - 1) & (NS - 1)
    last, head = tm == NT - 1, tm == NT - 2

    barrier = pltpu.get_barrier_semaphore()

    def greet(peer, slab):
        pl.semaphore_signal(barrier, inc=1, device_id=(peer, slab), device_id_type=MESH)

    greet(tm, up)
    greet(tm, down)
    for move in BESIDE:
        greet(moved(tm, *move), sp)
    middle = sp == MIDDLE

    @pl.when(middle)
    def _():
        for i in range(2, NS - 1):
            greet(tm, MIDDLE + i & (NS - 1))


    own = pl.ds(H, X)
    loads = [
        pltpu.make_async_copy(forcing, force.at[own], local_sem.at[1]),
        pltpu.make_async_copy(classes, walls.at[own], local_sem.at[2]),
        pltpu.make_async_copy(coarse, prop, local_sem.at[3]),
    ]
    field = pltpu.make_async_copy(guess.at[0], levels.at[0, own], local_sem.at[0])

    copy_table = pltpu.make_async_copy(damping_table, table, local_sem.at[5])

    def load():
        copy_table.start()
        for copy in loads:
            copy.start()
        pltpu.make_async_copy(initial, levels.at[9, own], local_sem.at[4]).start()

        @pl.when(last)
        def _():
            pltpu.make_async_copy(stale, levels.at[0, own], local_sem.at[0]).start()

        @pl.when(jnp.logical_not(last))
        def _():
            field.start()

    def keep_split(power, rows, value):
        first, second = split(value)
        high[power, rows, :] = first
        low[power, rows, :] = second

    def split_prop():
        loads[2].wait()

        def one(i, carry):
            rows = pl.ds(pl.multiple_of(i * 128, 128), 128)
            keep_split(0, rows, prop[rows, :])
            return carry

        lax.fori_loop(0, Z // 128, one, 0)

    def powers():
        for power in range(1, 4):
            def square(i, carry):
                rows = pl.ds(pl.multiple_of(i * BLOCK, BLOCK), BLOCK)
                first, second = high[power - 1, rows, :], low[power - 1, rows, :]
                value = (
                    jnp.dot(first, high[power - 1], preferred_element_type=F32)
                    + jnp.dot(first, low[power - 1], preferred_element_type=F32)
                    + jnp.dot(second, high[power - 1], preferred_element_type=F32)
                )
                keep_split(power, rows, value)
                return carry

            lax.fori_loop(0, Z // BLOCK, square, 0)

    early = sp < NS // 2

    @pl.when(early)
    def _():
        load()
        split_prop()
        powers()

    beside_middle = (sp >= MIDDLE - 1) & (sp <= MIDDLE + 1)
    pl.semaphore_wait(barrier, 2 + len(BESIDE) + jnp.where(beside_middle, 0, 1))

    def tell(index, slices, slabs):
        for peer in slices:
            for slab in slabs:
                pl.semaphore_signal(known.at[index], inc=1, device_id=(peer, slab), device_id_type=MESH)

    def halo(source, target, side, index, rows):
        if side == 0:
            here, there, slab = pl.ds(X - rows, rows), pl.ds(H - rows, rows), up
        else:
            here, there, slab = pl.ds(0, rows), pl.ds(H + X, rows), down
        return pltpu.make_async_remote_copy(
            src_ref=source.at[here], dst_ref=target.at[there],
            send_sem=halo_send.at[side, index], recv_sem=halo_recv.at[side, index],
            device_id=(tm, slab), device_id_type=MESH,
        )

    core = tm & 1
    other = tm ^ 1
    sides = (0, 1)
    for side in sides:
        @pl.when(core == 0)
        def _():
            halo(forcing, force, side, 1, 7).start()

        @pl.when(core == 1)
        def _():
            halo(classes, walls, side, 1, 7).start()

        @pl.when(last)
        def _():
            halo(stale, levels.at[0], side, 0, 8).start()

        @pl.when(jnp.logical_not(last))
        def _():
            halo(guess.at[0], levels.at[0], side, 0, 8).start()

        @pl.when(head)
        def _():
            halo(initial, levels.at[9], side, 3, 4).start()

    tell(0, [moved(tm, *move) for move in LINE], [sp])

    @pl.when(jnp.logical_not(early))
    def _():
        load()

    pl.semaphore_wait(known.at[0], len(LINE))

    @pl.when(jnp.logical_not(middle))
    def _():
        tell(1, [tm], [MIDDLE])

    @pl.when(jnp.logical_not(early))
    def _():
        split_prop()

    lane = lax.broadcasted_iota(jnp.int32, (1, Y, Z), 2)
    row = lax.broadcasted_iota(jnp.int32, (1, Y, Z), 1)
    not_left, not_right = lane > 0, lane < Z - 1
    not_first, not_final = row > 0, row < Y - 1

    def keep_factor(start, count):
        def one(i, carry):
            wall = walls[start + i]
            damping = jnp.zeros((Y, Z), F32)
            for class_no in range(4):
                damping = jnp.where(wall == class_no, table[class_no], damping)
            keep[start + i] = (1.0 - 6.0 * COUPLING) - damping
            return carry

        lax.fori_loop(0, count, one, 0)

    second_source = jnp.where(head, 9, 4)

    def step(level, start, count):
        source = second_source if level == 5 else level - 1

        def rows(at, size):
            field = levels[source, pl.ds(at, size)]
            around = levels[source, pl.ds(at - 1, size)] + levels[source, pl.ds(at + 1, size)]
            around += jnp.where(not_left, pltpu.roll(field, 1, 2), 0.0)
            around += jnp.where(not_right, pltpu.roll(field, Z - 1, 2), 0.0)
            around += jnp.where(not_first, pltpu.roll(field, 1, 1), 0.0)
            around += jnp.where(not_final, pltpu.roll(field, Y - 1, 1), 0.0)
            levels[level, pl.ds(at, size)] = (
                field * keep[pl.ds(at, size)] + COUPLING * around + force[pl.ds(at, size)]
            )

        for i in range(0, count, 4):
            rows(start + i, min(4, count - i))

    def end(side, count):
        return pl.ds(H - count, count) if side == 0 else pl.ds(H + X, count)

    def pass_on(side):
        there = end(side, 7)

        def onward(buffer):
            return pltpu.make_async_remote_copy(
                src_ref=buffer.at[there], dst_ref=buffer.at[there],
                send_sem=halo_send.at[side, 2], recv_sem=halo_recv.at[side, 2],
                device_id=(other, sp), device_id_type=MESH,
            )

        pltpu.make_async_copy(force.at[there], force.at[there], halo_recv.at[side, 1]).wait()

        @pl.when(core == 0)
        def _():
            onward(force).start()

        @pl.when(core == 1)
        def _():
            onward(walls).start()

    def wait_halo(side):
        for index, (buffer, count) in ((0, (levels.at[0], 8)), (2, (force, 7))):
            there = end(side, count)
            pltpu.make_async_copy(buffer.at[there], buffer.at[there], halo_recv.at[side, index]).wait()

        @pl.when(head)
        def _():
            there = end(side, 4)
            pltpu.make_async_copy(levels.at[9, there], levels.at[9, there], halo_recv.at[side, 3]).wait()

    def half_rows(half):
        return pl.ds(H + half * 8, 8)

    pieces = ((4, 8), (12, 4), (0, 4))

    def send_relaxed(piece):
        first, count = pieces[piece]
        pltpu.make_async_remote_copy(
            src_ref=levels.at[4, pl.ds(H + first, count)], dst_ref=beside.at[pl.ds(first, count)],
            send_sem=beside_send.at[piece], recv_sem=beside_recv.at[piece],
            device_id=((tm + NT - 1) & (NT - 1), sp), device_id_type=MESH,
        ).start()

    def send_half(half):
        relaxed = levels[4, half_rows(half)].reshape(64, Z)
        carried = product(relaxed, high[0], low[0]).reshape(8, Y, Z)
        term = levels[8, half_rows(half)] - jnp.where(head, 0.0, carried)
        for x in range(8):
            for k in range(4):
                outbox[half, pl.ds(x * 32 + k, 8, stride=4), :] = term[x, :, k * 128 : (k + 1) * 128]
        place = (tm + 2) & (NT - 1)
        pltpu.make_async_copy(
            outbox.at[half, pl.ds(pl.multiple_of(tm * 8, 8), 8)],
            scan.at[half, 0, pl.ds(pl.multiple_of((place + PAD) * 8, 8), 8)],
            own_sem.at[half, 0],
        ).start()
        for move in PEERS:
            peer = moved(tm, *move)
            pltpu.make_async_remote_copy(
                src_ref=outbox.at[half, pl.ds(pl.multiple_of(peer * 8, 8), 8)],
                dst_ref=scan.at[half, 0, pl.ds(pl.multiple_of((place + PAD) * 8, 8), 8)],
                send_sem=turn_send.at[half], recv_sem=turn_recv.at[half],
                device_id=(peer, sp), device_id_type=MESH,
            ).start()

    for copy in (copy_table, field, *loads[:2]):
        copy.wait()
    pltpu.make_async_copy(initial, levels.at[9, own], local_sem.at[4]).wait()
    for half in range(2):
        for stage in range(3):
            scan[half, stage, 0 : PAD * 8, :] = jnp.zeros((PAD * 8, 128), F32)
    keep_factor(H, X)
    for level in range(1, 8):
        step(level, H + level, X - 2 * level)
    send_relaxed(0)
    pass_on(1)
    pass_on(0)

    @pl.when(middle)
    def _():
        pl.semaphore_wait(known.at[1], NS - 1)
        tell(2, [tm], [slab for slab in range(NS) if slab != MIDDLE])

    wait_halo(1)
    keep_factor(H + X, 7)
    for level in range(1, 9):
        step(level, H + X - level, 8)
    send_relaxed(1)
    send_half(UPPER)
    wait_halo(0)
    keep_factor(1, 7)
    for level in range(1, 9):
        step(level, level, 8)
    send_relaxed(2)
    send_half(LOWER)

    total = jnp.zeros((Y, Z), F32)
    for piece, (first, count) in enumerate(pieces):
        rows = beside.at[pl.ds(first, count)]
        pltpu.make_async_copy(rows, rows, beside_recv.at[piece]).wait()

        def add(i, sums):
            residual = levels[8, H + i] - beside[i]
            return sums + residual * residual

        total = lax.fori_loop(first, first + count, add, total, unroll=True)
    lanes = total[:, 0:128] + total[:, 128:256] + total[:, 256:384] + total[:, 384:512]
    partial[...] = jnp.sum(lanes, axis=0, keepdims=True)
    @pl.when(jnp.logical_not(middle))
    def _():
        pl.semaphore_wait(known.at[2], 1)

    for i in range(NS):
        pltpu.make_async_remote_copy(
            src_ref=partial, dst_ref=gathered.at[sp], send_sem=norm_send, recv_sem=norm_recv,
            device_id=((tm + 2) & (NT - 1), (sp + i) & (NS - 1)), device_id_type=MESH,
        ).start()

    @pl.when(jnp.logical_not(early))
    def _():
        powers()

    def view(half, stage, first, slices):
        pieces = [
            scan[half, stage, pl.ds(first * 8 + k, slices * 2, stride=4), :] for k in range(4)
        ]
        return jnp.concatenate(pieces, axis=1)

    def store(buffer, first, slices, value):
        for k in range(4):
            buffer[pl.ds(first * 8 + k, slices * 2, stride=4), :] = value[:, k * 128 : (k + 1) * 128]

    for half in (UPPER, LOWER):
        mine = outbox.at[half, pl.ds(0, 8)]
        pltpu.make_async_copy(mine, mine, own_sem.at[half, 0]).wait()
        others = outbox.at[half, pl.ds(0, (NT - 1) * 8)]
        pltpu.make_async_copy(others, others, turn_recv.at[half]).wait()
        for stage in range(3):
            after = view(half, stage, PAD, NT) + product(
                view(half, stage, PAD - (1 << stage), NT), high[stage], low[stage]
            )
            if stage < 2:
                store(scan.at[half, stage + 1], PAD, NT, after)
        chunk = after[0:16]
        chunks = [chunk]
        for c in range(1, 4):
            chunk = after[c * 16 : (c + 1) * 16] + product(chunk, high[3], low[3])
            chunks.append(chunk)
        store(result.at[half], 0, NT, jnp.concatenate(chunks, axis=0))
        here = landed.at[pl.ds(pl.multiple_of(half * 256 + tm * 8, 8), 8)]
        pltpu.make_async_copy(
            result.at[half, pl.ds(pl.multiple_of(tm * 8, 8), 8)], here, own_sem.at[half, 1]
        ).start()
        for move in PEERS:
            peer = moved(tm, *move)
            pltpu.make_async_remote_copy(
                src_ref=result.at[half, pl.ds(pl.multiple_of(peer * 8, 8), 8)], dst_ref=here,
                send_sem=back_send.at[half], recv_sem=back_recv.at[half],
                device_id=(peer, sp), device_id_type=MESH,
            ).start()

    pltpu.make_async_copy(gathered, gathered, norm_recv).wait()
    squares = jnp.sum(gathered[...], axis=0)
    mean = jnp.sum(squares, axis=1, keepdims=True) / (NS * X * Y * Z)
    norm[...] = jnp.broadcast_to(jnp.sqrt(mean), (8, 128))

    for half in range(2):
        mine = outbox.at[half, pl.ds(0, 8)]
        others = outbox.at[half, pl.ds(0, (NT - 1) * 8)]
        pltpu.make_async_copy(mine, mine, own_sem.at[half, 1]).wait()
        pltpu.make_async_copy(others, others, back_recv.at[half]).wait()
        pltpu.make_async_copy(others, others, turn_send.at[half]).wait()
        pltpu.make_async_copy(others, others, back_send.at[half]).wait()
    pltpu.make_async_copy(gathered, gathered, norm_send).wait()
    for piece, (first, count) in enumerate(pieces):
        rows = beside.at[pl.ds(first, count)]
        pltpu.make_async_copy(rows, rows, beside_send.at[piece]).wait()
    for side in sides:
        for index, (buffer, count) in enumerate(((levels.at[0], 8), (force, 7), (force, 7))):
            there = pl.ds(0, count)
            pltpu.make_async_copy(buffer.at[there], buffer.at[there], halo_send.at[side, index]).wait()

        @pl.when(head)
        def _():
            there = pl.ds(0, 4)
            pltpu.make_async_copy(levels.at[9, there], levels.at[9, there], halo_send.at[side, 3]).wait()


def shards(initial, stale_start, guess, forcing, wall_class, damping_table, coarse_prop):
    anywhere = pl.BlockSpec(memory_space=pl.ANY)
    hbm = pl.BlockSpec(memory_space=pltpu.HBM)
    dma = pltpu.SemaphoreType.DMA
    landed, norm = pl.pallas_call(
        kernel,
        out_shape=(
            jax.ShapeDtypeStruct((X * Y * Z // 128, 128), F32),
            jax.ShapeDtypeStruct((8, 128), F32),
        ),
        in_specs=[hbm] * 7,
        out_specs=(anywhere, pl.BlockSpec(memory_space=pltpu.VMEM)),
        scratch_shapes=[
            pltpu.SMEM((4,), F32),
            pltpu.VMEM((10, X + 2 * H, Y, Z), F32),
            pltpu.VMEM((X + 2 * H, Y, Z), F32),
            pltpu.VMEM((X + 2 * H, Y, Z), jnp.int32),
            pltpu.VMEM((X + 2 * H, Y, Z), F32),
            pltpu.VMEM((Z, Z), F32),
            pltpu.VMEM((4, Z, Z), BF16),
            pltpu.VMEM((4, Z, Z), BF16),
            pltpu.VMEM((2, NT * 8, 128), F32),
            pltpu.VMEM((2, 3, (PAD + NT) * 8, 128), F32),
            pltpu.VMEM((2, NT * 8, 128), F32),
            pltpu.VMEM((X, Y, Z), F32),
            pltpu.VMEM((1, 128), F32),
            pltpu.VMEM((NS, 1, 128), F32),
            dma((6,)), dma((2, 4)), dma((2, 4)), dma((2,)), dma((2,)), dma((2,)), dma((2,)),
            dma((2, 2)), dma((3,)), dma((3,)), dma, dma, pltpu.SemaphoreType.REGULAR((3,)),
        ],
        compiler_params=pltpu.CompilerParams(
            collective_id=0, has_side_effects=True, vmem_limit_bytes=63 * 1024 * 1024
        ),
    )(initial, stale_start, guess, forcing, wall_class, damping_table, coarse_prop)
    return landed.reshape(1, X, Y, Z), norm[0, 0:1]


def solution(mesh):
    return jax.shard_map(
        shards,
        mesh=mesh,
        in_specs=(
            P("space", None, None),
            P("space", None, None),
            P("tm", "space", None, None),
            P("space", None, None),
            P("space", None, None),
            P(),
            P(),
        ),
        out_specs=(P("tm", "space", None, None), P("tm")),
        check_vma=False,
    )
```

```python
import functools

import jax
import jax.numpy as jnp
from jax import lax
from jax.experimental import pallas as pl
from jax.experimental.pallas import tpu as pltpu
from jax.sharding import PartitionSpec as P

MESH = pl.DeviceIdType.MESH
COUPLING = 0.12
F32, BF16 = jnp.float32, jnp.bfloat16
NT, NS = 32, 16
X, Y, Z = 16, 8, 512
HEAD, MIDDLE = 1, 4
H = 8
PAD = 4
BLOCK = 256
LOWER, UPPER = 0, 1


def split(value):
    high = value.astype(BF16)
    return high, (value - high.astype(F32)).astype(BF16)


def product(value, high, low):
    first, second = split(value)
    return (
        jnp.dot(first, high, preferred_element_type=F32)
        + jnp.dot(first, low, preferred_element_type=F32)
        + jnp.dot(second, high, preferred_element_type=F32)
    )


def moved(tm, dy, dx, dc):
    return ((tm + 8 * dy) & 24) | ((tm + 2 * dx) & 6) | ((tm ^ dc) & 1)


PEERS = sorted(
    [(dy, dx, dc) for dy in range(4) for dx in range(4) for dc in range(2)][1:],
    key=lambda d: -min(d[0], 4 - d[0]) - min(d[1], 4 - d[1]),
)
OTHER = (0, 0, 1)


def kernel(
    initial, stale, guess, forcing, classes, damping_table, coarse,
    landed, norm,
    table, levels, force, walls, keep, prop, high, low, outbox, scan, result, beside, partial, gathered,
    local_sem, halo_send, halo_recv, turn_send, turn_recv, back_send, back_recv, own_sem,
    beside_send, beside_recv, norm_send, norm_recv, known,
):
    tm, sp = lax.axis_index("tm"), lax.axis_index("space")
    up, down = (sp + 1) & (NS - 1), (sp + NS - 1) & (NS - 1)
    last, head = tm == NT - 1, tm == NT - 2

    barrier = pltpu.get_barrier_semaphore()

    def greet(peer, slab):
        pl.semaphore_signal(barrier, inc=1, device_id=(peer, slab), device_id_type=MESH)

    greet(tm, up)
    greet(tm, down)
    greet(tm ^ 1, sp)
    head_of_plane, middle = tm == HEAD, sp == MIDDLE

    @pl.when(head_of_plane)
    def _():
        for move in PEERS:
            if move != OTHER:
                greet(moved(tm, *move), sp)

        @pl.when(middle)
        def _():
            for i in range(2, NS - 1):
                greet(tm, MIDDLE + i & (NS - 1))

    first_in_line, last_in_line = (tm & 7) == 0, (tm & 7) == 7

    @pl.when(((tm & 1) == 1) & jnp.logical_not(last_in_line))
    def _():
        greet((tm + 1) & (NT - 1), sp)

    @pl.when(first_in_line)
    def _():
        greet((tm + NT - 1) & (NT - 1), sp)

    own = pl.ds(H, X)
    loads = [
        pltpu.make_async_copy(forcing, force.at[own], local_sem.at[1]),
        pltpu.make_async_copy(classes, walls.at[own], local_sem.at[2]),
        pltpu.make_async_copy(coarse, prop, local_sem.at[3]),
    ]
    field = pltpu.make_async_copy(guess.at[0], levels.at[0, own], local_sem.at[0])

    copy_table = pltpu.make_async_copy(damping_table, table, local_sem.at[5])

    def load():
        copy_table.start()
        for copy in loads:
            copy.start()
        pltpu.make_async_copy(initial, levels.at[9, own], local_sem.at[4]).start()

        @pl.when(last)
        def _():
            pltpu.make_async_copy(stale, levels.at[0, own], local_sem.at[0]).start()

        @pl.when(jnp.logical_not(last))
        def _():
            field.start()

    def keep_split(power, rows, value):
        first, second = split(value)
        high[power, rows, :] = first
        low[power, rows, :] = second

    def split_prop():
        loads[2].wait()

        def one(i, carry):
            rows = pl.ds(pl.multiple_of(i * 128, 128), 128)
            keep_split(0, rows, prop[rows, :])
            return carry

        lax.fori_loop(0, Z // 128, one, 0)

    def powers():
        for power in range(1, 4):
            def square(i, carry):
                rows = pl.ds(pl.multiple_of(i * BLOCK, BLOCK), BLOCK)
                first, second = high[power - 1, rows, :], low[power - 1, rows, :]
                value = (
                    jnp.dot(first, high[power - 1], preferred_element_type=F32)
                    + jnp.dot(first, low[power - 1], preferred_element_type=F32)
                    + jnp.dot(second, high[power - 1], preferred_element_type=F32)
                )
                keep_split(power, rows, value)
                return carry

            lax.fori_loop(0, Z // BLOCK, square, 0)

    early = sp < NS // 2

    @pl.when(early)
    def _():
        load()
        split_prop()
        powers()

    from_head = jnp.where((tm == HEAD) | (tm == HEAD ^ 1), 0, 1)
    from_middle = jnp.where(head_of_plane & ((sp < MIDDLE - 1) | (sp > MIDDLE + 1)), 1, 0)
    from_line = jnp.where((((tm & 1) == 0) & jnp.logical_not(first_in_line)) | last_in_line, 1, 0)
    pl.semaphore_wait(barrier, 3 + from_head + from_middle + from_line)

    def tell(index, slices, slabs):
        for peer in slices:
            for slab in slabs:
                pl.semaphore_signal(known.at[index], inc=1, device_id=(peer, slab), device_id_type=MESH)

    def halo(source, target, side, index, rows):
        if side == 0:
            here, there, slab = pl.ds(X - rows, rows), pl.ds(H - rows, rows), up
        else:
            here, there, slab = pl.ds(0, rows), pl.ds(H + X, rows), down
        return pltpu.make_async_remote_copy(
            src_ref=source.at[here], dst_ref=target.at[there],
            send_sem=halo_send.at[side, index], recv_sem=halo_recv.at[side, index],
            device_id=(tm, slab), device_id_type=MESH,
        )

    core = tm & 1
    other = tm ^ 1
    sides = (0, 1)
    for side in sides:
        @pl.when(core == 0)
        def _():
            halo(forcing, force, side, 1, 7).start()

        @pl.when(core == 1)
        def _():
            halo(classes, walls, side, 1, 7).start()

        @pl.when(last)
        def _():
            halo(stale, levels.at[0], side, 0, 8).start()

        @pl.when(jnp.logical_not(last))
        def _():
            halo(guess.at[0], levels.at[0], side, 0, 8).start()

        @pl.when(head)
        def _():
            halo(initial, levels.at[9], side, 3, 4).start()

    @pl.when(jnp.logical_not(head_of_plane))
    def _():
        tell(0, [HEAD], [sp])

    @pl.when(last_in_line)
    def _():
        tell(5, [(tm + 1) & (NT - 1)], [sp])

    plane = [moved(tm, *move) for move in PEERS]

    @pl.when(jnp.logical_not(early))
    def _():
        load()

    @pl.when(jnp.logical_not(early))
    def _():
        split_prop()

    lane = lax.broadcasted_iota(jnp.int32, (1, Y, Z), 2)
    row = lax.broadcasted_iota(jnp.int32, (1, Y, Z), 1)
    not_left, not_right = lane > 0, lane < Z - 1
    not_first, not_final = row > 0, row < Y - 1

    def keep_factor(start, count):
        def one(i, carry):
            wall = walls[start + i]
            damping = jnp.zeros((Y, Z), F32)
            for class_no in range(4):
                damping = jnp.where(wall == class_no, table[class_no], damping)
            keep[start + i] = (1.0 - 6.0 * COUPLING) - damping
            return carry

        lax.fori_loop(0, count, one, 0)

    second_source = jnp.where(head, 9, 4)

    def step(level, start, count):
        source = second_source if level == 5 else level - 1

        def rows(at, size):
            field = levels[source, pl.ds(at, size)]
            around = levels[source, pl.ds(at - 1, size)] + levels[source, pl.ds(at + 1, size)]
            around += jnp.where(not_left, pltpu.roll(field, 1, 2), 0.0)
            around += jnp.where(not_right, pltpu.roll(field, Z - 1, 2), 0.0)
            around += jnp.where(not_first, pltpu.roll(field, 1, 1), 0.0)
            around += jnp.where(not_final, pltpu.roll(field, Y - 1, 1), 0.0)
            levels[level, pl.ds(at, size)] = (
                field * keep[pl.ds(at, size)] + COUPLING * around + force[pl.ds(at, size)]
            )

        for i in range(0, count, 4):
            rows(start + i, min(4, count - i))

    def end(side, count):
        return pl.ds(H - count, count) if side == 0 else pl.ds(H + X, count)

    def pass_on(side):
        there = end(side, 7)

        def onward(buffer):
            return pltpu.make_async_remote_copy(
                src_ref=buffer.at[there], dst_ref=buffer.at[there],
                send_sem=halo_send.at[side, 2], recv_sem=halo_recv.at[side, 2],
                device_id=(other, sp), device_id_type=MESH,
            )

        pltpu.make_async_copy(force.at[there], force.at[there], halo_recv.at[side, 1]).wait()

        @pl.when(core == 0)
        def _():
            onward(force).start()

        @pl.when(core == 1)
        def _():
            onward(walls).start()

    def wait_halo(side):
        for index, (buffer, count) in ((0, (levels.at[0], 8)), (2, (force, 7))):
            there = end(side, count)
            pltpu.make_async_copy(buffer.at[there], buffer.at[there], halo_recv.at[side, index]).wait()

        @pl.when(head)
        def _():
            there = end(side, 4)
            pltpu.make_async_copy(levels.at[9, there], levels.at[9, there], halo_recv.at[side, 3]).wait()

    def half_rows(half):
        return pl.ds(H + half * 8, 8)

    pieces = ((4, 8), (12, 4), (0, 4))

    def send_relaxed(piece):
        first, count = pieces[piece]
        pltpu.make_async_remote_copy(
            src_ref=levels.at[4, pl.ds(H + first, count)], dst_ref=beside.at[pl.ds(first, count)],
            send_sem=beside_send.at[piece], recv_sem=beside_recv.at[piece],
            device_id=((tm + NT - 1) & (NT - 1), sp), device_id_type=MESH,
        ).start()

    def send_half(half):
        relaxed = levels[4, half_rows(half)].reshape(64, Z)
        carried = product(relaxed, high[0], low[0]).reshape(8, Y, Z)
        term = levels[8, half_rows(half)] - jnp.where(head, 0.0, carried)
        for x in range(8):
            for k in range(4):
                outbox[half, pl.ds(x * 32 + k, 8, stride=4), :] = term[x, :, k * 128 : (k + 1) * 128]
        place = (tm + 2) & (NT - 1)
        pltpu.make_async_copy(
            outbox.at[half, pl.ds(pl.multiple_of(tm * 8, 8), 8)],
            scan.at[half, 0, pl.ds(pl.multiple_of((place + PAD) * 8, 8), 8)],
            own_sem.at[half, 0],
        ).start()
        for move in PEERS:
            peer = moved(tm, *move)
            pltpu.make_async_remote_copy(
                src_ref=outbox.at[half, pl.ds(pl.multiple_of(peer * 8, 8), 8)],
                dst_ref=scan.at[half, 0, pl.ds(pl.multiple_of((place + PAD) * 8, 8), 8)],
                send_sem=turn_send.at[half], recv_sem=turn_recv.at[half],
                device_id=(peer, sp), device_id_type=MESH,
            ).start()

    for copy in (copy_table, field, *loads[:2]):
        copy.wait()
    pltpu.make_async_copy(initial, levels.at[9, own], local_sem.at[4]).wait()
    for half in range(2):
        for stage in range(3):
            scan[half, stage, 0 : PAD * 8, :] = jnp.zeros((PAD * 8, 128), F32)
    keep_factor(H, X)
    for level in range(1, 8):
        step(level, H + level, X - 2 * level)
    @pl.when(first_in_line)
    def _():
        pl.semaphore_wait(known.at[5], 1)

    send_relaxed(0)
    pass_on(1)
    pass_on(0)

    @pl.when(head_of_plane)
    def _():
        pl.semaphore_wait(known.at[0], NT - 1)
        tell(1, plane, [sp])

        @pl.when(jnp.logical_not(middle))
        def _():
            tell(2, [HEAD], [MIDDLE])

    wait_halo(1)
    keep_factor(H + X, 7)
    for level in range(1, 9):
        step(level, H + X - level, 8)
    send_relaxed(1)

    @pl.when(jnp.logical_not(head_of_plane))
    def _():
        pl.semaphore_wait(known.at[1], 1)

    send_half(UPPER)
    wait_halo(0)
    keep_factor(1, 7)
    for level in range(1, 9):
        step(level, level, 8)
    send_relaxed(2)
    send_half(LOWER)

    @pl.when(head_of_plane)
    def _():
        @pl.when(middle)
        def _():
            pl.semaphore_wait(known.at[2], NS - 1)
            tell(3, [HEAD], [slab for slab in range(NS) if slab != MIDDLE])

        @pl.when(jnp.logical_not(middle))
        def _():
            pl.semaphore_wait(known.at[3], 1)

        tell(4, plane, [sp])

    total = jnp.zeros((Y, Z), F32)
    for piece, (first, count) in enumerate(pieces):
        rows = beside.at[pl.ds(first, count)]
        pltpu.make_async_copy(rows, rows, beside_recv.at[piece]).wait()

        def add(i, sums):
            residual = levels[8, H + i] - beside[i]
            return sums + residual * residual

        total = lax.fori_loop(first, first + count, add, total, unroll=True)
    lanes = total[:, 0:128] + total[:, 128:256] + total[:, 256:384] + total[:, 384:512]
    partial[...] = jnp.sum(lanes, axis=0, keepdims=True)
    @pl.when(jnp.logical_not(head_of_plane))
    def _():
        pl.semaphore_wait(known.at[4], 1)

    for i in range(NS):
        pltpu.make_async_remote_copy(
            src_ref=partial, dst_ref=gathered.at[sp], send_sem=norm_send, recv_sem=norm_recv,
            device_id=((tm + 2) & (NT - 1), (sp + i) & (NS - 1)), device_id_type=MESH,
        ).start()

    @pl.when(jnp.logical_not(early))
    def _():
        powers()

    def view(half, stage, first, slices):
        pieces = [
            scan[half, stage, pl.ds(first * 8 + k, slices * 2, stride=4), :] for k in range(4)
        ]
        return jnp.concatenate(pieces, axis=1)

    def store(buffer, first, slices, value):
        for k in range(4):
            buffer[pl.ds(first * 8 + k, slices * 2, stride=4), :] = value[:, k * 128 : (k + 1) * 128]

    for half in (UPPER, LOWER):
        mine = outbox.at[half, pl.ds(0, 8)]
        pltpu.make_async_copy(mine, mine, own_sem.at[half, 0]).wait()
        others = outbox.at[half, pl.ds(0, (NT - 1) * 8)]
        pltpu.make_async_copy(others, others, turn_recv.at[half]).wait()
        for stage in range(3):
            after = view(half, stage, PAD, NT) + product(
                view(half, stage, PAD - (1 << stage), NT), high[stage], low[stage]
            )
            if stage < 2:
                store(scan.at[half, stage + 1], PAD, NT, after)
        chunk = after[0:16]
        chunks = [chunk]
        for c in range(1, 4):
            chunk = after[c * 16 : (c + 1) * 16] + product(chunk, high[3], low[3])
            chunks.append(chunk)
        store(result.at[half], 0, NT, jnp.concatenate(chunks, axis=0))
        here = landed.at[pl.ds(pl.multiple_of(half * 256 + tm * 8, 8), 8)]
        pltpu.make_async_copy(
            result.at[half, pl.ds(pl.multiple_of(tm * 8, 8), 8)], here, own_sem.at[half, 1]
        ).start()
        for move in PEERS:
            peer = moved(tm, *move)
            pltpu.make_async_remote_copy(
                src_ref=result.at[half, pl.ds(pl.multiple_of(peer * 8, 8), 8)], dst_ref=here,
                send_sem=back_send.at[half], recv_sem=back_recv.at[half],
                device_id=(peer, sp), device_id_type=MESH,
            ).start()

    pltpu.make_async_copy(gathered, gathered, norm_recv).wait()
    squares = jnp.sum(gathered[...], axis=0)
    mean = jnp.sum(squares, axis=1, keepdims=True) / (NS * X * Y * Z)
    norm[...] = jnp.broadcast_to(jnp.sqrt(mean), (8, 128))

    for half in range(2):
        mine = outbox.at[half, pl.ds(0, 8)]
        others = outbox.at[half, pl.ds(0, (NT - 1) * 8)]
        pltpu.make_async_copy(mine, mine, own_sem.at[half, 1]).wait()
        pltpu.make_async_copy(others, others, back_recv.at[half]).wait()
        pltpu.make_async_copy(others, others, turn_send.at[half]).wait()
        pltpu.make_async_copy(others, others, back_send.at[half]).wait()
    pltpu.make_async_copy(gathered, gathered, norm_send).wait()
    for piece, (first, count) in enumerate(pieces):
        rows = beside.at[pl.ds(first, count)]
        pltpu.make_async_copy(rows, rows, beside_send.at[piece]).wait()
    for side in sides:
        for index, (buffer, count) in enumerate(((levels.at[0], 8), (force, 7), (force, 7))):
            there = pl.ds(0, count)
            pltpu.make_async_copy(buffer.at[there], buffer.at[there], halo_send.at[side, index]).wait()

        @pl.when(head)
        def _():
            there = pl.ds(0, 4)
            pltpu.make_async_copy(levels.at[9, there], levels.at[9, there], halo_send.at[side, 3]).wait()


def shards(initial, stale_start, guess, forcing, wall_class, damping_table, coarse_prop):
    anywhere = pl.BlockSpec(memory_space=pl.ANY)
    hbm = pl.BlockSpec(memory_space=pltpu.HBM)
    dma = pltpu.SemaphoreType.DMA
    landed, norm = pl.pallas_call(
        kernel,
        out_shape=(
            jax.ShapeDtypeStruct((X * Y * Z // 128, 128), F32),
            jax.ShapeDtypeStruct((8, 128), F32),
        ),
        in_specs=[hbm] * 7,
        out_specs=(anywhere, pl.BlockSpec(memory_space=pltpu.VMEM)),
        scratch_shapes=[
            pltpu.SMEM((4,), F32),
            pltpu.VMEM((10, X + 2 * H, Y, Z), F32),
            pltpu.VMEM((X + 2 * H, Y, Z), F32),
            pltpu.VMEM((X + 2 * H, Y, Z), jnp.int32),
            pltpu.VMEM((X + 2 * H, Y, Z), F32),
            pltpu.VMEM((Z, Z), F32),
            pltpu.VMEM((4, Z, Z), BF16),
            pltpu.VMEM((4, Z, Z), BF16),
            pltpu.VMEM((2, NT * 8, 128), F32),
            pltpu.VMEM((2, 3, (PAD + NT) * 8, 128), F32),
            pltpu.VMEM((2, NT * 8, 128), F32),
            pltpu.VMEM((X, Y, Z), F32),
            pltpu.VMEM((1, 128), F32),
            pltpu.VMEM((NS, 1, 128), F32),
            dma((6,)), dma((2, 4)), dma((2, 4)), dma((2,)), dma((2,)), dma((2,)), dma((2,)),
            dma((2, 2)), dma((3,)), dma((3,)), dma, dma, pltpu.SemaphoreType.REGULAR((6,)),
        ],
        compiler_params=pltpu.CompilerParams(
            collective_id=0, has_side_effects=True, vmem_limit_bytes=54900 * 1024
        ),
    )(initial, stale_start, guess, forcing, wall_class, damping_table, coarse_prop)
    return landed.reshape(1, X, Y, Z), norm[0, 0:1]


def solution(mesh):
    return jax.shard_map(
        shards,
        mesh=mesh,
        in_specs=(
            P("space", None, None),
            P("space", None, None),
            P("tm", "space", None, None),
            P("space", None, None),
            P("space", None, None),
            P(),
            P(),
        ),
        out_specs=(P("tm", "space", None, None), P("tm")),
        check_vma=False,
    )
```

```python
import functools

import jax
import jax.numpy as jnp
from jax import lax
from jax.experimental import pallas as pl
from jax.experimental.pallas import tpu as pltpu
from jax.sharding import PartitionSpec as P

MESH = pl.DeviceIdType.MESH
COUPLING = 0.12
F32, BF16 = jnp.float32, jnp.bfloat16
NT, NS = 32, 16
X, Y, Z = 16, 8, 512
FIRST = 4
HEAD, MIDDLE = 1, 4
H = 8
PAD = 4
BLOCK = 256
LOWER, UPPER = 0, 1


def split(value):
    high = value.astype(BF16)
    return high, (value - high.astype(F32)).astype(BF16)


def product(value, high, low):
    first, second = split(value)
    return (
        jnp.dot(first, high, preferred_element_type=F32)
        + jnp.dot(first, low, preferred_element_type=F32)
        + jnp.dot(second, high, preferred_element_type=F32)
    )


def moved(tm, dy, dx, dc):
    return ((tm + 8 * dy) & 24) | ((tm + 2 * dx) & 6) | ((tm ^ dc) & 1)


PEERS = sorted(
    [(dy, dx, dc) for dy in range(4) for dx in range(4) for dc in range(2)][1:],
    key=lambda d: -min(d[0], 4 - d[0]) - min(d[1], 4 - d[1]),
)
OTHER = (0, 0, 1)


def kernel(
    initial, stale, guess, forcing, classes, damping_table, coarse,
    landed, norm,
    table, levels, force, walls, keep, prop, high, low, outbox, scan, result, beside, partial, gathered,
    local_sem, halo_send, halo_recv, turn_send, turn_recv, back_send, back_recv, own_sem,
    beside_send, beside_recv, norm_send, norm_recv, known,
):
    tm, sp = lax.axis_index("tm"), lax.axis_index("space")
    up, down = (sp + 1) & (NS - 1), (sp + NS - 1) & (NS - 1)
    last, head = tm == NT - 1, tm == NT - 2

    barrier = pltpu.get_barrier_semaphore()

    def greet(peer, slab):
        pl.semaphore_signal(barrier, inc=1, device_id=(peer, slab), device_id_type=MESH)

    greet(tm, up)
    greet(tm, down)
    greet(tm ^ 1, sp)
    head_of_plane, middle = tm == HEAD, sp == MIDDLE

    @pl.when(head_of_plane)
    def _():
        for move in PEERS:
            if move != OTHER:
                greet(moved(tm, *move), sp)

        @pl.when(middle)
        def _():
            for i in range(2, NS - 1):
                greet(tm, MIDDLE + i & (NS - 1))

    first_slabs, early = sp < FIRST, sp < NS // 2

    @pl.when(first_slabs)
    def _():
        for slab in range(FIRST, NS):
            greet((tm + NT - 2) & (NT - 1), slab)

    first_in_line, last_in_line = (tm & 7) == 0, (tm & 7) == 7

    @pl.when(((tm & 1) == 1) & jnp.logical_not(last_in_line))
    def _():
        greet((tm + 1) & (NT - 1), sp)

    @pl.when(first_in_line)
    def _():
        greet((tm + NT - 1) & (NT - 1), sp)

    own = pl.ds(H, X)
    loads = [
        pltpu.make_async_copy(forcing, force.at[own], local_sem.at[1]),
        pltpu.make_async_copy(classes, walls.at[own], local_sem.at[2]),
        pltpu.make_async_copy(coarse, prop, local_sem.at[3]),
    ]
    field = pltpu.make_async_copy(guess.at[0], levels.at[0, own], local_sem.at[0])

    copy_table = pltpu.make_async_copy(damping_table, table, local_sem.at[5])

    def load():
        copy_table.start()
        for copy in loads:
            copy.start()
        @pl.when(head)
        def _():
            pltpu.make_async_copy(initial, levels.at[9, own], local_sem.at[4]).start()

        @pl.when(last)
        def _():
            pltpu.make_async_copy(stale, levels.at[0, own], local_sem.at[0]).start()

        @pl.when(jnp.logical_not(last))
        def _():
            field.start()

    def keep_split(power, rows, value):
        first, second = split(value)
        high[power, rows, :] = first
        low[power, rows, :] = second

    def split_prop():
        loads[2].wait()

        def one(i, carry):
            rows = pl.ds(pl.multiple_of(i * 128, 128), 128)
            keep_split(0, rows, prop[rows, :])
            return carry

        lax.fori_loop(0, Z // 128, one, 0)

    def powers(first, end):
        for power in range(first, end):
            def square(i, carry):
                rows = pl.ds(pl.multiple_of(i * BLOCK, BLOCK), BLOCK)
                first, second = high[power - 1, rows, :], low[power - 1, rows, :]
                value = (
                    jnp.dot(first, high[power - 1], preferred_element_type=F32)
                    + jnp.dot(first, low[power - 1], preferred_element_type=F32)
                    + jnp.dot(second, high[power - 1], preferred_element_type=F32)
                )
                keep_split(power, rows, value)
                return carry

            lax.fori_loop(0, Z // BLOCK, square, 0)

    @pl.when(early)
    def _():
        load()
        split_prop()
        powers(1, 4)

    from_head = jnp.where((tm == HEAD) | (tm == HEAD ^ 1), 0, 1)
    from_middle = jnp.where(head_of_plane & ((sp < MIDDLE - 1) | (sp > MIDDLE + 1)), 1, 0)
    from_line = jnp.where((((tm & 1) == 0) & jnp.logical_not(first_in_line)) | last_in_line, 1, 0)
    pl.semaphore_wait(barrier, 3 + from_head + from_middle + from_line + jnp.where(first_slabs, 0, FIRST))

    def tell(index, slices, slabs):
        for peer in slices:
            for slab in slabs:
                pl.semaphore_signal(known.at[index], inc=1, device_id=(peer, slab), device_id_type=MESH)

    def halo(source, target, side, index, rows):
        if side == 0:
            here, there, slab = pl.ds(X - rows, rows), pl.ds(H - rows, rows), up
        else:
            here, there, slab = pl.ds(0, rows), pl.ds(H + X, rows), down
        return pltpu.make_async_remote_copy(
            src_ref=source.at[here], dst_ref=target.at[there],
            send_sem=halo_send.at[side, index], recv_sem=halo_recv.at[side, index],
            device_id=(tm, slab), device_id_type=MESH,
        )

    core = tm & 1
    other = tm ^ 1
    sides = (0, 1)
    for side in sides:
        @pl.when(core == 0)
        def _():
            halo(forcing, force, side, 1, 7).start()

        @pl.when(core == 1)
        def _():
            halo(classes, walls, side, 1, 7).start()

        @pl.when(last)
        def _():
            halo(stale, levels.at[0], side, 0, 8).start()

        @pl.when(jnp.logical_not(last))
        def _():
            halo(guess.at[0], levels.at[0], side, 0, 8).start()

        @pl.when(head)
        def _():
            halo(initial, levels.at[9], side, 3, 4).start()

    @pl.when(jnp.logical_not(head_of_plane))
    def _():
        tell(0, [HEAD], [sp])

    @pl.when(last_in_line)
    def _():
        tell(5, [(tm + 1) & (NT - 1)], [sp])

    plane = [moved(tm, *move) for move in PEERS]

    @pl.when(jnp.logical_not(early))
    def _():
        load()

    @pl.when(jnp.logical_not(early))
    def _():
        split_prop()
        powers(1, 3)

    lane = lax.broadcasted_iota(jnp.int32, (1, Y, Z), 2)
    row = lax.broadcasted_iota(jnp.int32, (1, Y, Z), 1)
    not_left, not_right = lane > 0, lane < Z - 1
    not_first, not_final = row > 0, row < Y - 1

    def keep_factor(start, count):
        def one(i, carry):
            wall = walls[start + i]
            damping = jnp.zeros((Y, Z), F32)
            for class_no in range(4):
                damping = jnp.where(wall == class_no, table[class_no], damping)
            keep[start + i] = (1.0 - 6.0 * COUPLING) - damping
            return carry

        lax.fori_loop(0, count, one, 0, unroll=True)

    second_source = jnp.where(head, 9, 4)

    def step(level, start, count):
        source = second_source if level == 5 else level - 1

        def rows(at, size):
            field = levels[source, pl.ds(at, size)]
            around = levels[source, pl.ds(at - 1, size)] + levels[source, pl.ds(at + 1, size)]
            around += jnp.where(not_left, pltpu.roll(field, 1, 2), 0.0)
            around += jnp.where(not_right, pltpu.roll(field, Z - 1, 2), 0.0)
            around += jnp.where(not_first, pltpu.roll(field, 1, 1), 0.0)
            around += jnp.where(not_final, pltpu.roll(field, Y - 1, 1), 0.0)
            levels[level, pl.ds(at, size)] = (
                field * keep[pl.ds(at, size)] + COUPLING * around + force[pl.ds(at, size)]
            )

        for i in range(0, count, 4):
            rows(start + i, min(4, count - i))

    def end(side, count):
        return pl.ds(H - count, count) if side == 0 else pl.ds(H + X, count)

    def pass_on(side):
        there = end(side, 7)

        def onward(buffer):
            return pltpu.make_async_remote_copy(
                src_ref=buffer.at[there], dst_ref=buffer.at[there],
                send_sem=halo_send.at[side, 2], recv_sem=halo_recv.at[side, 2],
                device_id=(other, sp), device_id_type=MESH,
            )

        pltpu.make_async_copy(force.at[there], force.at[there], halo_recv.at[side, 1]).wait()

        @pl.when(core == 0)
        def _():
            onward(force).start()

        @pl.when(core == 1)
        def _():
            onward(walls).start()

    def wait_statics(side):
        there = end(side, 7)
        pltpu.make_async_copy(force.at[there], force.at[there], halo_recv.at[side, 2]).wait()
        keep_factor(H + X if side == 1 else 1, 7)

    def wait_field(side):
        there = end(side, 8)
        pltpu.make_async_copy(levels.at[0, there], levels.at[0, there], halo_recv.at[side, 0]).wait()

        @pl.when(head)
        def _():
            there = end(side, 4)
            pltpu.make_async_copy(levels.at[9, there], levels.at[9, there], halo_recv.at[side, 3]).wait()

    def half_rows(half):
        return pl.ds(H + half * 8, 8)

    pieces = ((4, 8), (12, 4), (0, 4))

    def send_relaxed(piece):
        first, count = pieces[piece]
        pltpu.make_async_remote_copy(
            src_ref=levels.at[4, pl.ds(H + first, count)], dst_ref=beside.at[pl.ds(first, count)],
            send_sem=beside_send.at[piece], recv_sem=beside_recv.at[piece],
            device_id=((tm + NT - 1) & (NT - 1), sp), device_id_type=MESH,
        ).start()

    def send_half(half):
        relaxed = levels[4, half_rows(half)].reshape(64, Z)
        carried = product(relaxed, high[0], low[0]).reshape(8, Y, Z)
        term = levels[8, half_rows(half)] - jnp.where(head, 0.0, carried)
        for x in range(8):
            for k in range(4):
                outbox[half, pl.ds(x * 32 + k, 8, stride=4), :] = term[x, :, k * 128 : (k + 1) * 128]
        place = (tm + 2) & (NT - 1)
        pltpu.make_async_copy(
            outbox.at[half, pl.ds(pl.multiple_of(tm * 8, 8), 8)],
            scan.at[half, 0, pl.ds(pl.multiple_of((place + PAD) * 8, 8), 8)],
            own_sem.at[half, 0],
        ).start()
        for move in PEERS:
            peer = moved(tm, *move)
            pltpu.make_async_remote_copy(
                src_ref=outbox.at[half, pl.ds(pl.multiple_of(peer * 8, 8), 8)],
                dst_ref=scan.at[half, 0, pl.ds(pl.multiple_of((place + PAD) * 8, 8), 8)],
                send_sem=turn_send.at[half], recv_sem=turn_recv.at[half],
                device_id=(peer, sp), device_id_type=MESH,
            ).start()

    for copy in (copy_table, field, *loads[:2]):
        copy.wait()

    @pl.when(head)
    def _():
        pltpu.make_async_copy(initial, levels.at[9, own], local_sem.at[4]).wait()

    for half in range(2):
        for stage in range(3):
            scan[half, stage, 0 : PAD * 8, :] = jnp.zeros((PAD * 8, 128), F32)
    keep_factor(H, X)
    for level in range(1, 8):
        step(level, H + level, X - 2 * level)
    @pl.when(first_in_line)
    def _():
        pl.semaphore_wait(known.at[5], 1)

    send_relaxed(0)
    pass_on(1)
    pass_on(0)

    @pl.when(head_of_plane)
    def _():
        pl.semaphore_wait(known.at[0], NT - 1)
        tell(1, plane, [sp])

        @pl.when(jnp.logical_not(middle))
        def _():
            tell(2, [HEAD], [MIDDLE])

    def steps(side, first, last):
        for level in range(first, last + 1):
            step(level, H + X - level if side == 1 else level, 8)

    def first_sweep(side):
        wait_field(side)
        steps(side, 1, 4)
        send_relaxed(1 if side == 1 else 2)

    def hear_plane():
        @pl.when(jnp.logical_not(head_of_plane))
        def _():
            pl.semaphore_wait(known.at[1], 1)

    def pass_world():
        @pl.when(head_of_plane)
        def _():
            @pl.when(jnp.logical_not(middle))
            def _():
                pl.semaphore_wait(known.at[3], 1)

            tell(4, plane, [sp])

    @pl.when(early)
    def _():
        wait_statics(1)
        first_sweep(1)
        steps(1, 5, 8)
        hear_plane()
        send_half(UPPER)

        @pl.when(head_of_plane & middle)
        def _():
            pl.semaphore_wait(known.at[2], NS - 1)
            tell(3, [HEAD], [slab for slab in range(NS) if slab != MIDDLE])

        wait_statics(0)
        first_sweep(0)
        steps(0, 5, 8)
        send_half(LOWER)

    @pl.when(jnp.logical_not(early))
    def _():
        wait_statics(1)
        wait_statics(0)
        first_sweep(1)
        first_sweep(0)
        steps(1, 5, 8)
        hear_plane()
        send_half(UPPER)
        pass_world()
        steps(0, 5, 8)
        send_half(LOWER)

    def sum_squares():
        total = jnp.zeros((Y, Z), F32)
        for piece, (first, count) in enumerate(pieces):
            rows = beside.at[pl.ds(first, count)]
            pltpu.make_async_copy(rows, rows, beside_recv.at[piece]).wait()

            def add(i, sums):
                residual = levels[8, H + i] - beside[i]
                return sums + residual * residual

            total = lax.fori_loop(first, first + count, add, total, unroll=True)
        lanes = total[:, 0:128] + total[:, 128:256] + total[:, 256:384] + total[:, 384:512]
        partial[...] = jnp.sum(lanes, axis=0, keepdims=True)

    def send_squares(slabs):
        for slab in slabs:
            pltpu.make_async_remote_copy(
                src_ref=partial, dst_ref=gathered.at[sp], send_sem=norm_send, recv_sem=norm_recv,
                device_id=((tm + 2) & (NT - 1), slab), device_id_type=MESH,
            ).start()

    def hear_all():
        @pl.when(jnp.logical_not(head_of_plane))
        def _():
            pl.semaphore_wait(known.at[4], 1)

    @pl.when(jnp.logical_not(first_slabs))
    def _():
        sum_squares()
        send_squares(range(FIRST))

    @pl.when(early)
    def _():
        pass_world()

    @pl.when(jnp.logical_not(early))
    def _():
        powers(3, 4)

    @pl.when(jnp.logical_not(first_slabs))
    def _():
        hear_all()
        send_squares(range(FIRST, NS))

    def view(half, stage, first, slices):
        pieces = [
            scan[half, stage, pl.ds(first * 8 + k, slices * 2, stride=4), :] for k in range(4)
        ]
        return jnp.concatenate(pieces, axis=1)

    def store(buffer, first, slices, value):
        for k in range(4):
            buffer[pl.ds(first * 8 + k, slices * 2, stride=4), :] = value[:, k * 128 : (k + 1) * 128]

    for half in (UPPER, LOWER):
        mine = outbox.at[half, pl.ds(0, 8)]
        pltpu.make_async_copy(mine, mine, own_sem.at[half, 0]).wait()
        others = outbox.at[half, pl.ds(0, (NT - 1) * 8)]
        pltpu.make_async_copy(others, others, turn_recv.at[half]).wait()
        for stage in range(3):
            after = view(half, stage, PAD, NT) + product(
                view(half, stage, PAD - (1 << stage), NT), high[stage], low[stage]
            )
            if stage < 2:
                store(scan.at[half, stage + 1], PAD, NT, after)
        chunk = after[0:16]
        chunks = [chunk]
        for c in range(1, 4):
            chunk = after[c * 16 : (c + 1) * 16] + product(chunk, high[3], low[3])
            chunks.append(chunk)
        store(result.at[half], 0, NT, jnp.concatenate(chunks, axis=0))
        here = landed.at[pl.ds(pl.multiple_of(half * 256 + tm * 8, 8), 8)]
        pltpu.make_async_copy(
            result.at[half, pl.ds(pl.multiple_of(tm * 8, 8), 8)], here, own_sem.at[half, 1]
        ).start()
        for move in PEERS:
            peer = moved(tm, *move)
            pltpu.make_async_remote_copy(
                src_ref=result.at[half, pl.ds(pl.multiple_of(peer * 8, 8), 8)], dst_ref=here,
                send_sem=back_send.at[half], recv_sem=back_recv.at[half],
                device_id=(peer, sp), device_id_type=MESH,
            ).start()

    @pl.when(first_slabs)
    def _():
        sum_squares()
        hear_all()
        send_squares(range(NS))

    pltpu.make_async_copy(gathered, gathered, norm_recv).wait()
    squares = jnp.sum(gathered[...], axis=0)
    mean = jnp.sum(squares, axis=1, keepdims=True) / (NS * X * Y * Z)
    norm[...] = jnp.broadcast_to(jnp.sqrt(mean), (8, 128))

    for half in range(2):
        mine = outbox.at[half, pl.ds(0, 8)]
        others = outbox.at[half, pl.ds(0, (NT - 1) * 8)]
        pltpu.make_async_copy(mine, mine, own_sem.at[half, 1]).wait()
        pltpu.make_async_copy(others, others, back_recv.at[half]).wait()
        pltpu.make_async_copy(others, others, turn_send.at[half]).wait()
        pltpu.make_async_copy(others, others, back_send.at[half]).wait()
    pltpu.make_async_copy(gathered, gathered, norm_send).wait()
    for piece, (first, count) in enumerate(pieces):
        rows = beside.at[pl.ds(first, count)]
        pltpu.make_async_copy(rows, rows, beside_send.at[piece]).wait()
    for side in sides:
        for index, (buffer, count) in enumerate(((levels.at[0], 8), (force, 7), (force, 7))):
            there = pl.ds(0, count)
            pltpu.make_async_copy(buffer.at[there], buffer.at[there], halo_send.at[side, index]).wait()

        @pl.when(head)
        def _():
            there = pl.ds(0, 4)
            pltpu.make_async_copy(levels.at[9, there], levels.at[9, there], halo_send.at[side, 3]).wait()


def shards(initial, stale_start, guess, forcing, wall_class, damping_table, coarse_prop):
    anywhere = pl.BlockSpec(memory_space=pl.ANY)
    hbm = pl.BlockSpec(memory_space=pltpu.HBM)
    dma = pltpu.SemaphoreType.DMA
    landed, norm = pl.pallas_call(
        kernel,
        out_shape=(
            jax.ShapeDtypeStruct((X * Y * Z // 128, 128), F32),
            jax.ShapeDtypeStruct((8, 128), F32),
        ),
        in_specs=[hbm] * 7,
        out_specs=(anywhere, pl.BlockSpec(memory_space=pltpu.VMEM)),
        scratch_shapes=[
            pltpu.SMEM((4,), F32),
            pltpu.VMEM((10, X + 2 * H, Y, Z), F32),
            pltpu.VMEM((X + 2 * H, Y, Z), F32),
            pltpu.VMEM((X + 2 * H, Y, Z), jnp.int32),
            pltpu.VMEM((X + 2 * H, Y, Z), F32),
            pltpu.VMEM((Z, Z), F32),
            pltpu.VMEM((4, Z, Z), BF16),
            pltpu.VMEM((4, Z, Z), BF16),
            pltpu.VMEM((2, NT * 8, 128), F32),
            pltpu.VMEM((2, 3, (PAD + NT) * 8, 128), F32),
            pltpu.VMEM((2, NT * 8, 128), F32),
            pltpu.VMEM((X, Y, Z), F32),
            pltpu.VMEM((1, 128), F32),
            pltpu.VMEM((NS, 1, 128), F32),
            dma((6,)), dma((2, 4)), dma((2, 4)), dma((2,)), dma((2,)), dma((2,)), dma((2,)),
            dma((2, 2)), dma((3,)), dma((3,)), dma, dma, pltpu.SemaphoreType.REGULAR((6,)),
        ],
        compiler_params=pltpu.CompilerParams(
            collective_id=0, has_side_effects=True, vmem_limit_bytes=54900 * 1024
        ),
    )(initial, stale_start, guess, forcing, wall_class, damping_table, coarse_prop)
    return landed.reshape(1, X, Y, Z), norm[0, 0:1]


def solution(mesh):
    return jax.shard_map(
        shards,
        mesh=mesh,
        in_specs=(
            P("space", None, None),
            P("space", None, None),
            P("tm", "space", None, None),
            P("space", None, None),
            P("space", None, None),
            P(),
            P(),
        ),
        out_specs=(P("tm", "space", None, None), P("tm")),
        check_vma=False,
    )
```

```python
import functools

import jax
import jax.numpy as jnp
from jax import lax
from jax.experimental import pallas as pl
from jax.experimental.pallas import tpu as pltpu
from jax.sharding import PartitionSpec as P

MESH = pl.DeviceIdType.MESH
COUPLING = 0.12
F32, BF16 = jnp.float32, jnp.bfloat16
NT, NS = 32, 16
X, Y, Z = 16, 8, 512
FIRST = 4
HEAD, MIDDLE = 1, 4
H = 8
PAD = 4
BLOCK = 256
LOWER, UPPER = 0, 1


def split(value):
    high = value.astype(BF16)
    return high, (value - high.astype(F32)).astype(BF16)


def product(value, high, low):
    first, second = split(value)
    return (
        jnp.dot(first, high, preferred_element_type=F32)
        + jnp.dot(first, low, preferred_element_type=F32)
        + jnp.dot(second, high, preferred_element_type=F32)
    )


def moved(tm, dy, dx, dc):
    return ((tm + 8 * dy) & 24) | ((tm + 2 * dx) & 6) | ((tm ^ dc) & 1)


PEERS = sorted(
    [(dy, dx, dc) for dy in range(4) for dx in range(4) for dc in range(2)][1:],
    key=lambda d: -min(d[0], 4 - d[0]) - min(d[1], 4 - d[1]),
)
OTHER = (0, 0, 1)


def kernel(
    initial, stale, guess, forcing, classes, damping_table, coarse,
    landed, norm,
    table, levels, force, walls, keep, prop, high, low, outbox, scan, result, beside, partial, gathered,
    local_sem, halo_send, halo_recv, turn_send, turn_recv, back_send, back_recv, own_sem,
    beside_send, beside_recv, norm_send, norm_recv, known,
):
    tm, sp = lax.axis_index("tm"), lax.axis_index("space")
    up, down = (sp + 1) & (NS - 1), (sp + NS - 1) & (NS - 1)
    last, head = tm == NT - 1, tm == NT - 2

    barrier = pltpu.get_barrier_semaphore()

    def greet(peer, slab):
        pl.semaphore_signal(barrier, inc=1, device_id=(peer, slab), device_id_type=MESH)

    greet(tm, up)
    greet(tm, down)
    greet(tm ^ 1, sp)
    head_of_plane, middle = tm == HEAD, sp == MIDDLE

    @pl.when(head_of_plane)
    def _():
        for move in PEERS:
            if move != OTHER:
                greet(moved(tm, *move), sp)

        @pl.when(middle)
        def _():
            for i in range(2, NS - 1):
                greet(tm, MIDDLE + i & (NS - 1))

    first_slabs, early = sp < FIRST, sp < NS // 2

    @pl.when(first_slabs)
    def _():
        for slab in range(FIRST, NS):
            greet((tm + NT - 2) & (NT - 1), slab)

    first_in_line, last_in_line = (tm & 7) == 0, (tm & 7) == 7

    @pl.when(((tm & 1) == 1) & jnp.logical_not(last_in_line))
    def _():
        greet((tm + 1) & (NT - 1), sp)

    @pl.when(first_in_line)
    def _():
        greet((tm + NT - 1) & (NT - 1), sp)

    own = pl.ds(H, X)
    loads = [
        pltpu.make_async_copy(forcing, force.at[own], local_sem.at[1]),
        pltpu.make_async_copy(classes, walls.at[own], local_sem.at[2]),
        pltpu.make_async_copy(coarse, prop, local_sem.at[3]),
    ]
    field = pltpu.make_async_copy(guess.at[0], levels.at[0, own], local_sem.at[0])

    copy_table = pltpu.make_async_copy(damping_table, table, local_sem.at[5])

    def load():
        copy_table.start()
        for copy in loads:
            copy.start()
        @pl.when(head)
        def _():
            pltpu.make_async_copy(initial, levels.at[9, own], local_sem.at[4]).start()

        @pl.when(last)
        def _():
            pltpu.make_async_copy(stale, levels.at[0, own], local_sem.at[0]).start()

        @pl.when(jnp.logical_not(last))
        def _():
            field.start()

    def keep_split(power, rows, value):
        first, second = split(value)
        high[power, rows, :] = first
        low[power, rows, :] = second

    def split_prop():
        loads[2].wait()

        def one(i, carry):
            rows = pl.ds(pl.multiple_of(i * 128, 128), 128)
            keep_split(0, rows, prop[rows, :])
            return carry

        lax.fori_loop(0, Z // 128, one, 0)

    def powers(first, end):
        for power in range(first, end):
            def square(i, carry):
                rows = pl.ds(pl.multiple_of(i * BLOCK, BLOCK), BLOCK)
                first, second = high[power - 1, rows, :], low[power - 1, rows, :]
                value = (
                    jnp.dot(first, high[power - 1], preferred_element_type=F32)
                    + jnp.dot(first, low[power - 1], preferred_element_type=F32)
                    + jnp.dot(second, high[power - 1], preferred_element_type=F32)
                )
                keep_split(power, rows, value)
                return carry

            lax.fori_loop(0, Z // BLOCK, square, 0)

    @pl.when(early)
    def _():
        load()
        split_prop()
        powers(1, 4)

    from_head = jnp.where((tm == HEAD) | (tm == HEAD ^ 1), 0, 1)
    from_middle = jnp.where(head_of_plane & ((sp < MIDDLE - 1) | (sp > MIDDLE + 1)), 1, 0)
    from_line = jnp.where((((tm & 1) == 0) & jnp.logical_not(first_in_line)) | last_in_line, 1, 0)
    pl.semaphore_wait(barrier, 3 + from_head + from_middle + from_line + jnp.where(first_slabs, 0, FIRST))

    def tell(index, slices, slabs):
        for peer in slices:
            for slab in slabs:
                pl.semaphore_signal(known.at[index], inc=1, device_id=(peer, slab), device_id_type=MESH)

    def halo(source, target, side, index, rows):
        if side == 0:
            here, there, slab = pl.ds(X - rows, rows), pl.ds(H - rows, rows), up
        else:
            here, there, slab = pl.ds(0, rows), pl.ds(H + X, rows), down
        return pltpu.make_async_remote_copy(
            src_ref=source.at[here], dst_ref=target.at[there],
            send_sem=halo_send.at[side, index], recv_sem=halo_recv.at[side, index],
            device_id=(tm, slab), device_id_type=MESH,
        )

    core = tm & 1
    other = tm ^ 1
    sides = (0, 1)
    for side in sides:
        @pl.when(core == 0)
        def _():
            halo(forcing, force, side, 1, 7).start()

        @pl.when(core == 1)
        def _():
            halo(classes, walls, side, 1, 7).start()

        @pl.when(last)
        def _():
            halo(stale, levels.at[0], side, 0, 8).start()

        @pl.when(jnp.logical_not(last))
        def _():
            halo(guess.at[0], levels.at[0], side, 0, 8).start()

        @pl.when(head)
        def _():
            halo(initial, levels.at[9], side, 3, 4).start()

    @pl.when(jnp.logical_not(head_of_plane))
    def _():
        tell(0, [HEAD], [sp])

    @pl.when(last_in_line)
    def _():
        tell(5, [(tm + 1) & (NT - 1)], [sp])

    plane = [moved(tm, *move) for move in PEERS]

    @pl.when(jnp.logical_not(early))
    def _():
        load()

    @pl.when(jnp.logical_not(early))
    def _():
        split_prop()
        powers(1, 3)

    lane = lax.broadcasted_iota(jnp.int32, (1, Y, Z), 2)
    row = lax.broadcasted_iota(jnp.int32, (1, Y, Z), 1)
    not_left, not_right = lane > 0, lane < Z - 1
    not_first, not_final = row > 0, row < Y - 1

    def keep_factor(start, count):
        def one(i, carry):
            wall = walls[start + i]
            damping = jnp.zeros((Y, Z), F32)
            for class_no in range(4):
                damping = jnp.where(wall == class_no, table[class_no], damping)
            keep[start + i] = (1.0 - 6.0 * COUPLING) - damping
            return carry

        lax.fori_loop(0, count, one, 0, unroll=True)

    second_source = jnp.where(head, 9, 4)

    def step(level, start, count):
        source = second_source if level == 5 else level - 1

        def rows(at, size):
            field = levels[source, pl.ds(at, size)]
            around = levels[source, pl.ds(at - 1, size)] + levels[source, pl.ds(at + 1, size)]
            around += jnp.where(not_left, pltpu.roll(field, 1, 2), 0.0)
            around += jnp.where(not_right, pltpu.roll(field, Z - 1, 2), 0.0)
            around += jnp.where(not_first, pltpu.roll(field, 1, 1), 0.0)
            around += jnp.where(not_final, pltpu.roll(field, Y - 1, 1), 0.0)
            levels[level, pl.ds(at, size)] = (
                field * keep[pl.ds(at, size)] + COUPLING * around + force[pl.ds(at, size)]
            )

        for i in range(0, count, 4):
            rows(start + i, min(4, count - i))

    def end(side, count):
        return pl.ds(H - count, count) if side == 0 else pl.ds(H + X, count)

    def pass_on(side):
        there = end(side, 7)

        def onward(buffer):
            return pltpu.make_async_remote_copy(
                src_ref=buffer.at[there], dst_ref=buffer.at[there],
                send_sem=halo_send.at[side, 2], recv_sem=halo_recv.at[side, 2],
                device_id=(other, sp), device_id_type=MESH,
            )

        pltpu.make_async_copy(force.at[there], force.at[there], halo_recv.at[side, 1]).wait()

        @pl.when(core == 0)
        def _():
            onward(force).start()

        @pl.when(core == 1)
        def _():
            onward(walls).start()

    def wait_statics(side):
        there = end(side, 7)
        pltpu.make_async_copy(force.at[there], force.at[there], halo_recv.at[side, 2]).wait()
        keep_factor(H + X if side == 1 else 1, 7)

    def wait_field(side):
        there = end(side, 8)
        pltpu.make_async_copy(levels.at[0, there], levels.at[0, there], halo_recv.at[side, 0]).wait()

        @pl.when(head)
        def _():
            there = end(side, 4)
            pltpu.make_async_copy(levels.at[9, there], levels.at[9, there], halo_recv.at[side, 3]).wait()

    def half_rows(half):
        return pl.ds(H + half * 8, 8)

    pieces = ((4, 8), (12, 4), (0, 4))

    def send_relaxed(piece):
        first, count = pieces[piece]
        pltpu.make_async_remote_copy(
            src_ref=levels.at[4, pl.ds(H + first, count)], dst_ref=beside.at[pl.ds(first, count)],
            send_sem=beside_send.at[piece], recv_sem=beside_recv.at[piece],
            device_id=((tm + NT - 1) & (NT - 1), sp), device_id_type=MESH,
        ).start()

    def send_half(half):
        relaxed = levels[4, half_rows(half)].reshape(64, Z)
        carried = product(relaxed, high[0], low[0]).reshape(8, Y, Z)
        term = levels[8, half_rows(half)] - jnp.where(head, 0.0, carried)
        for x in range(8):
            for k in range(4):
                outbox[half, pl.ds(x * 32 + k, 8, stride=4), :] = term[x, :, k * 128 : (k + 1) * 128]
        place = (tm + 2) & (NT - 1)
        pltpu.make_async_copy(
            outbox.at[half, pl.ds(pl.multiple_of(tm * 8, 8), 8)],
            scan.at[half, 0, pl.ds(pl.multiple_of((place + PAD) * 8, 8), 8)],
            own_sem.at[half, 0],
        ).start()
        for move in PEERS:
            peer = moved(tm, *move)
            pltpu.make_async_remote_copy(
                src_ref=outbox.at[half, pl.ds(pl.multiple_of(peer * 8, 8), 8)],
                dst_ref=scan.at[half, 0, pl.ds(pl.multiple_of((place + PAD) * 8, 8), 8)],
                send_sem=turn_send.at[half], recv_sem=turn_recv.at[half],
                device_id=(peer, sp), device_id_type=MESH,
            ).start()

    for copy in (copy_table, field, *loads[:2]):
        copy.wait()

    @pl.when(head)
    def _():
        pltpu.make_async_copy(initial, levels.at[9, own], local_sem.at[4]).wait()

    for half in range(2):
        for stage in range(3):
            scan[half, stage, 0 : PAD * 8, :] = jnp.zeros((PAD * 8, 128), F32)
    keep_factor(H, X)
    for level in range(1, 8):
        step(level, H + level, X - 2 * level)
    @pl.when(first_in_line)
    def _():
        pl.semaphore_wait(known.at[5], 1)

    send_relaxed(0)
    pass_on(1)
    pass_on(0)

    @pl.when(head_of_plane)
    def _():
        pl.semaphore_wait(known.at[0], NT - 1)
        tell(1, plane, [sp])

        @pl.when(jnp.logical_not(middle))
        def _():
            tell(2, [HEAD], [MIDDLE])

    def steps(side, first, last):
        for level in range(first, last + 1):
            step(level, H + X - level if side == 1 else level, 8)

    def first_sweep(side):
        wait_field(side)
        steps(side, 1, 4)
        send_relaxed(1 if side == 1 else 2)

    def hear_plane():
        @pl.when(jnp.logical_not(head_of_plane))
        def _():
            pl.semaphore_wait(known.at[1], 1)

    def pass_world():
        @pl.when(head_of_plane)
        def _():
            @pl.when(jnp.logical_not(middle))
            def _():
                pl.semaphore_wait(known.at[3], 1)

            tell(4, plane, [sp])

    def sum_squares():
        total = jnp.zeros((Y, Z), F32)
        for piece, (first, count) in enumerate(pieces):
            rows = beside.at[pl.ds(first, count)]
            pltpu.make_async_copy(rows, rows, beside_recv.at[piece]).wait()

            def add(i, sums):
                residual = levels[8, H + i] - beside[i]
                return sums + residual * residual

            total = lax.fori_loop(first, first + count, add, total, unroll=True)
        lanes = total[:, 0:128] + total[:, 128:256] + total[:, 256:384] + total[:, 384:512]
        partial[...] = jnp.sum(lanes, axis=0, keepdims=True)

    def send_squares(slabs):
        for slab in slabs:
            pltpu.make_async_remote_copy(
                src_ref=partial, dst_ref=gathered.at[sp], send_sem=norm_send, recv_sem=norm_recv,
                device_id=((tm + 2) & (NT - 1), slab), device_id_type=MESH,
            ).start()

    @pl.when(early)
    def _():
        wait_statics(1)
        first_sweep(1)
        steps(1, 5, 8)
        hear_plane()
        send_half(UPPER)

        @pl.when(head_of_plane & middle)
        def _():
            pl.semaphore_wait(known.at[2], NS - 1)
            tell(3, [HEAD], [slab for slab in range(NS) if slab != MIDDLE])

        wait_statics(0)
        first_sweep(0)
        steps(0, 5, 8)
        send_half(LOWER)

    @pl.when(jnp.logical_not(early))
    def _():
        wait_statics(1)
        wait_statics(0)
        first_sweep(1)
        first_sweep(0)
        steps(1, 5, 8)
        steps(0, 5, 8)
        sum_squares()
        send_squares(range(FIRST))
        hear_plane()
        send_half(UPPER)
        pass_world()
        send_half(LOWER)

    def hear_all():
        @pl.when(jnp.logical_not(head_of_plane))
        def _():
            pl.semaphore_wait(known.at[4], 1)

    @pl.when(early & jnp.logical_not(first_slabs))
    def _():
        sum_squares()
        send_squares(range(FIRST))

    @pl.when(early)
    def _():
        pass_world()

    @pl.when(jnp.logical_not(early))
    def _():
        powers(3, 4)

    @pl.when(jnp.logical_not(first_slabs))
    def _():
        hear_all()
        send_squares(range(FIRST, NS))

    def view(half, stage, first, slices):
        pieces = [
            scan[half, stage, pl.ds(first * 8 + k, slices * 2, stride=4), :] for k in range(4)
        ]
        return jnp.concatenate(pieces, axis=1)

    def store(buffer, first, slices, value):
        for k in range(4):
            buffer[pl.ds(first * 8 + k, slices * 2, stride=4), :] = value[:, k * 128 : (k + 1) * 128]

    for half in (UPPER, LOWER):
        mine = outbox.at[half, pl.ds(0, 8)]
        pltpu.make_async_copy(mine, mine, own_sem.at[half, 0]).wait()
        others = outbox.at[half, pl.ds(0, (NT - 1) * 8)]
        pltpu.make_async_copy(others, others, turn_recv.at[half]).wait()
        for stage in range(3):
            after = view(half, stage, PAD, NT) + product(
                view(half, stage, PAD - (1 << stage), NT), high[stage], low[stage]
            )
            if stage < 2:
                store(scan.at[half, stage + 1], PAD, NT, after)
        chunk = after[0:16]
        chunks = [chunk]
        for c in range(1, 4):
            chunk = after[c * 16 : (c + 1) * 16] + product(chunk, high[3], low[3])
            chunks.append(chunk)
        store(result.at[half], 0, NT, jnp.concatenate(chunks, axis=0))
        here = landed.at[pl.ds(pl.multiple_of(half * 256 + tm * 8, 8), 8)]
        pltpu.make_async_copy(
            result.at[half, pl.ds(pl.multiple_of(tm * 8, 8), 8)], here, own_sem.at[half, 1]
        ).start()
        for move in PEERS:
            peer = moved(tm, *move)
            pltpu.make_async_remote_copy(
                src_ref=result.at[half, pl.ds(pl.multiple_of(peer * 8, 8), 8)], dst_ref=here,
                send_sem=back_send.at[half], recv_sem=back_recv.at[half],
                device_id=(peer, sp), device_id_type=MESH,
            ).start()

    @pl.when(first_slabs)
    def _():
        sum_squares()
        hear_all()
        send_squares(range(NS))

    pltpu.make_async_copy(gathered, gathered, norm_recv).wait()
    squares = jnp.sum(gathered[...], axis=0)
    mean = jnp.sum(squares, axis=1, keepdims=True) / (NS * X * Y * Z)
    norm[...] = jnp.broadcast_to(jnp.sqrt(mean), (8, 128))

    for half in range(2):
        mine = outbox.at[half, pl.ds(0, 8)]
        others = outbox.at[half, pl.ds(0, (NT - 1) * 8)]
        pltpu.make_async_copy(mine, mine, own_sem.at[half, 1]).wait()
        pltpu.make_async_copy(others, others, back_recv.at[half]).wait()
        pltpu.make_async_copy(others, others, turn_send.at[half]).wait()
        pltpu.make_async_copy(others, others, back_send.at[half]).wait()
    pltpu.make_async_copy(gathered, gathered, norm_send).wait()
    for piece, (first, count) in enumerate(pieces):
        rows = beside.at[pl.ds(first, count)]
        pltpu.make_async_copy(rows, rows, beside_send.at[piece]).wait()
    for side in sides:
        for index, (buffer, count) in enumerate(((levels.at[0], 8), (force, 7), (force, 7))):
            there = pl.ds(0, count)
            pltpu.make_async_copy(buffer.at[there], buffer.at[there], halo_send.at[side, index]).wait()

        @pl.when(head)
        def _():
            there = pl.ds(0, 4)
            pltpu.make_async_copy(levels.at[9, there], levels.at[9, there], halo_send.at[side, 3]).wait()


def shards(initial, stale_start, guess, forcing, wall_class, damping_table, coarse_prop):
    anywhere = pl.BlockSpec(memory_space=pl.ANY)
    hbm = pl.BlockSpec(memory_space=pltpu.HBM)
    dma = pltpu.SemaphoreType.DMA
    landed, norm = pl.pallas_call(
        kernel,
        out_shape=(
            jax.ShapeDtypeStruct((X * Y * Z // 128, 128), F32),
            jax.ShapeDtypeStruct((8, 128), F32),
        ),
        in_specs=[hbm] * 7,
        out_specs=(anywhere, pl.BlockSpec(memory_space=pltpu.VMEM)),
        scratch_shapes=[
            pltpu.SMEM((4,), F32),
            pltpu.VMEM((10, X + 2 * H, Y, Z), F32),
            pltpu.VMEM((X + 2 * H, Y, Z), F32),
            pltpu.VMEM((X + 2 * H, Y, Z), jnp.int32),
            pltpu.VMEM((X + 2 * H, Y, Z), F32),
            pltpu.VMEM((Z, Z), F32),
            pltpu.VMEM((4, Z, Z), BF16),
            pltpu.VMEM((4, Z, Z), BF16),
            pltpu.VMEM((2, NT * 8, 128), F32),
            pltpu.VMEM((2, 3, (PAD + NT) * 8, 128), F32),
            pltpu.VMEM((2, NT * 8, 128), F32),
            pltpu.VMEM((X, Y, Z), F32),
            pltpu.VMEM((1, 128), F32),
            pltpu.VMEM((NS, 1, 128), F32),
            dma((6,)), dma((2, 4)), dma((2, 4)), dma((2,)), dma((2,)), dma((2,)), dma((2,)),
            dma((2, 2)), dma((3,)), dma((3,)), dma, dma, pltpu.SemaphoreType.REGULAR((6,)),
        ],
        compiler_params=pltpu.CompilerParams(
            collective_id=0, has_side_effects=True, vmem_limit_bytes=54900 * 1024
        ),
    )(initial, stale_start, guess, forcing, wall_class, damping_table, coarse_prop)
    return landed.reshape(1, X, Y, Z), norm[0, 0:1]


def solution(mesh):
    return jax.shard_map(
        shards,
        mesh=mesh,
        in_specs=(
            P("space", None, None),
            P("space", None, None),
            P("tm", "space", None, None),
            P("space", None, None),
            P("space", None, None),
            P(),
            P(),
        ),
        out_specs=(P("tm", "space", None, None), P("tm")),
        check_vma=False,
    )
```
